256 devices in a mesh: branch: 2 (over core), seq: 8 (over y, x_lo), dp: 16 (over x_hi, z).
Axes of the slice: x: 4 (x_hi: 2, x_lo: 2; x = x_hi * 2 + x_lo), y: 4, z: 8, core: 2. Of those that a mesh axis runs over, the one named last changes fastest.
Arguments:
- context: bfloat16 [16, 1024, 5120], P('dp', 'seq', 'branch'), may hold values from -6 to 6
- main_stream: bfloat16 [16, 1024, 5120], P('dp', 'seq'), may hold values from -6 to 6
- cell_order: int32 [16, 1024], P('dp', 'seq'), may hold values from 0 to 1023, each once within a row
- modulation: float32 [16, 2, 5120], P('dp'), may hold values from -3 to 3
- hint_weight: bfloat16 [5120, 5120], P(('branch', 'dp'), 'seq'), may hold values from -0.078125 to 0.078125
- hint_bias: float32 [5120], P('seq'), may hold values from -3 to 3
- weights: bfloat16 [2, 5120, 5120], P('branch', 'dp', 'seq'), may hold values from -2 to 2
- biases: float32 [2, 5120], P('branch', 'seq'), may hold values from -3 to 3
- norm_gains: float32 [2, 5120], P('branch', 'seq'), may hold values from 0.25 to 1.75
Outputs:
- projections: bfloat16 [2, 16, 1024, 5120], P('branch', 'dp', None, 'seq')
- main_next: bfloat16 [16, 1024, 5120], P('dp', 'seq', 'branch')
The draws below stay inside these ranges and needn't reach their ends.
Inputs may be any that keep to these rules, and one draw needn't show every extreme that they name: `cell_order`: each row lists every one of the 1024 cells of the window once.
All inputs are finite; a program needn't handle non-finite values.
Results may differ from the reference program's by a relative error of at most 0.006.
Values may be sent and summed in bfloat16 or wider, within the bound.
No kernel may reach another device: no remote copies, remote signals or barrier semaphores. Data moves between devices by JAX's collectives and lax.ppermute only.
A program may use at most 128 MiB of HBM per device.

```python
import math
import jax
import jax.numpy as jnp
from jax import lax

D = 5120
HEAD = 128
TILE_H = 8
TILE_W = 16
TOKENS = 1024
SAMPLES = 16


def draw_weights(key, part):
    key = jax.random.fold_in(key, 7)
    key_base, key_head, key_column = jax.random.split(key, 3)
    head_count = D // HEAD
    rising = jnp.sqrt(1.0 + 3.0 * jnp.arange(head_count, dtype=jnp.float32) / (head_count - 1))
    base_draw = jnp.clip(jax.random.normal(key_base, (2, D, D), jnp.float32), -4.0, 4.0)
    head_spread = jnp.exp(jax.random.uniform(key_head, (2, 1, head_count), jnp.float32, -0.7, 0.7))
    head_scale = jnp.repeat(rising[None, None, :] * head_spread, HEAD, axis=2)
    column_scale = jnp.exp(jax.random.uniform(key_column, (2, 1, D), jnp.float32, -0.45, 0.45))
    return (base_draw * head_scale * column_scale * (0.5 / math.sqrt(D))).astype(jnp.bfloat16)


def block_scale(stream_key, dims, cuts, least, largest):
    loudness, own = 1.0, jax.random.fold_in(stream_key, 6)
    for dim, blocks in cuts:
        steps = jnp.exp(jax.random.uniform(jax.random.fold_in(own, dim), (blocks,), jnp.float32, least / len(cuts), largest / len(cuts)))
        loudness = loudness * jnp.repeat(steps, dims[dim] // blocks).reshape([-1 if axis == dim else 1 for axis in range(len(dims))])
    return loudness


def gaussian(stream_key, shape, width, reach, shards=(), held_as=jnp.bfloat16):
    gain = block_scale(stream_key, shape, shards, -0.22, 0.18) if shards else 1.0
    drawn = jax.random.normal(stream_key, shape, jnp.float32) * width * gain
    return jnp.minimum(jnp.maximum(drawn, -reach), reach).astype(held_as)


def setup_inputs(seed: int = 0) -> dict:
    key_of = jax.random.split(jax.random.key(seed), 10)
    return {
        "context": gaussian(key_of[0], (SAMPLES, TOKENS, D), 1.0, 6.0, ((0, 16), (1, 8), (2, 2))),
        "main_stream": gaussian(key_of[1], (SAMPLES, TOKENS, D), 1.0, 6.0, ((0, 16), (1, 8))),
        "cell_order": jax.vmap(lambda own: jax.random.permutation(own, TOKENS))(jax.random.split(key_of[2], SAMPLES)).reshape((SAMPLES, TOKENS)).astype(jnp.int32),
        "modulation": gaussian(key_of[3], (SAMPLES, 2, D), 0.5, 3.0, ((0, 16),), jnp.float32),
        "hint_weight": gaussian(key_of[4], (D, D), D ** -0.5, 0.078125, ((0, 32), (1, 8))),
        "hint_bias": gaussian(key_of[5], (D,), 0.5, 3.0, ((0, 8),), jnp.float32),
        "weights": draw_weights(jax.random.fold_in(key_of[9], 71), 0),
        "biases": gaussian(key_of[7], (2, D), 0.5, 3.0, ((0, 2), (1, 8)), jnp.float32),
        "norm_gains": jnp.clip(1.0 + 0.15 * jax.random.normal(key_of[8], (2, D), jnp.float32), 0.25, 1.75),
    }


norm_eps = 1e-06

def modulate(token_rows, shift_scale):
    values = token_rows.astype(jnp.float32)
    average = lax.optimization_barrier(jnp.mean(values, axis=-1, keepdims=True))
    centered = values - average
    variance = lax.optimization_barrier(jnp.mean(centered * centered, axis=-1, keepdims=True))
    normed = centered * lax.rsqrt(variance + norm_eps)
    return (normed * (1.0 + shift_scale[1]) + shift_scale[0]).astype(jnp.bfloat16)

def rope_tables(cell_ids):
    half_head = HEAD // 2
    sixth_head = HEAD // 6
    frame_pairs = half_head - 2 * sixth_head
    pair_index = jnp.arange(half_head, dtype=jnp.int32)
    in_frame = pair_index < frame_pairs
    in_height = jnp.logical_and(pair_index >= frame_pairs, pair_index < frame_pairs + sixth_head)
    local_index = jnp.where(in_frame, pair_index, jnp.where(in_height, pair_index - frame_pairs, pair_index - frame_pairs - sixth_head))
    section = jnp.where(in_frame, frame_pairs, sixth_head)
    frequency = jnp.power(10000.0, -local_index.astype(jnp.float32) / section.astype(jnp.float32))
    frame_ids = cell_ids // (TILE_H * TILE_W)
    row_ids = cell_ids // TILE_W % TILE_H
    col_ids = cell_ids % TILE_W
    position = jnp.where(in_frame[None, :], frame_ids[:, None], jnp.where(in_height[None, :], row_ids[:, None], col_ids[:, None]))
    angles = position.astype(jnp.float32) * frequency[None, :]
    return (jnp.cos(angles), jnp.sin(angles))

def rotate(values, cosine, sine_tab):
    num_rows, features = values.shape
    paired = values.reshape(num_rows, features // HEAD, HEAD // 2, 2)
    even_part = paired[..., 0]
    odd_part = paired[..., 1]
    cos_wide = cosine[:, None, :]
    sin_wide = sine_tab[:, None, :]
    turned = jnp.stack([even_part * cos_wide - odd_part * sin_wide, even_part * sin_wide + odd_part * cos_wide], axis=-1)
    return turned.reshape(num_rows, features)

def reference(context, main_stream, cell_order, modulation, hint_weight, hint_bias, weights, biases, norm_gains):

    def one_sample(inputs):
        context_rows, main_rows, cell_ids, shift_scale = inputs
        hint = (jnp.dot(context_rows, hint_weight, preferred_element_type=jnp.float32) + hint_bias).astype(jnp.bfloat16)
        mixed = (main_rows.astype(jnp.float32) + hint.astype(jnp.float32)).astype(jnp.bfloat16)
        normed = modulate(mixed, shift_scale)
        cosine, sine_tab = rope_tables(cell_ids)
        results = []
        for slot_index in range(2):
            projected = jnp.dot(normed, weights[slot_index], preferred_element_type=jnp.float32) + biases[slot_index]
            mean_square = lax.optimization_barrier(jnp.mean(projected * projected, axis=-1, keepdims=True))
            scaled = projected * lax.rsqrt(mean_square + norm_eps) * norm_gains[slot_index]
            results.append(rotate(scaled, cosine, sine_tab).astype(jnp.bfloat16))
        return (jnp.stack(results), mixed)
    stacked, main_next = lax.map(one_sample, (context, main_stream, cell_order, modulation))
    return (jnp.transpose(stacked, (1, 0, 2, 3)), main_next)
```

```python
import functools

import jax
import jax.numpy as jnp
from jax import lax
from jax.experimental import pallas as pl
from jax.experimental.pallas import tpu as pltpu
from jax.sharding import PartitionSpec as P

HEAD = 128
TILE_H = 8
TILE_W = 16
norm_eps = 1e-06

F32 = jnp.float32
BF16 = jnp.bfloat16

NY, NX, NH, NZ = 4, 2, 2, 8
NS = NY * NX
SWAP = [(0, 1), (1, 0)]
REL = [(0, 0), (-1, 0), (1, 0), (0, 1), (2, 0), (1, 1), (-1, 1), (2, 1)]
Z_GROUPS = [[hh * NZ + z for z in range(NZ)] for hh in range(NH)]
SC_AFTER = 0


def seq_pairs(dy, dx):
    return [(s, ((s // NX + dy) % NY) * NX + (s % NX ^ dx)) for s in range(NS)]


def dp_pairs(dh, dz):
    return [(d, (d // NZ ^ dh) * NZ + (d % NZ + dz) % NZ) for d in range(NH * NZ)]


def seq_send(x, dy, dx):
    return lax.ppermute(x, "seq", seq_pairs(dy, dx))


def dp_send(x, dh, dz):
    return lax.ppermute(x, "dp", dp_pairs(dh, dz))


def core_swap(x):
    return lax.ppermute(x, "branch", SWAP)


def thirds(rows):
    unit = rows // 16
    first = -(-unit // 3)
    second = -(-(unit - first) // 2)
    return first * 16, (first + second) * 16


def after(value, *earlier):
    return lax.optimization_barrier((value, earlier))[0]


def cat(*parts):
    return jnp.concatenate(parts, 0)


def relay_mixed(own, beside_first, beside_second):
    rows = own.shape[0]
    half = rows // 2
    cut_a, cut_b = thirds(rows)
    back, ahead, beside, extra = lax.optimization_barrier(
        (seq_send(own, 1, 0), seq_send(own, -1, 0), seq_send(own, 0, 1), beside_first())
    )
    up, down, over, extra = lax.optimization_barrier(
        (
            seq_send(cat(back[:half], beside[half:]), 1, 0),
            seq_send(cat(beside[:half], ahead[half:]), -1, 0),
            seq_send(cat(back[:half], ahead[half:]), 0, 1),
            beside_second(extra),
        )
    )
    last = (
        seq_send(up[:cut_a], 0, 1),
        seq_send(cat(over[cut_a:half], up[half:cut_b]), 1, 0),
        seq_send(over[cut_b:], -1, 0),
    )
    arrays = [own, back, ahead, beside, up, down, over, *last]
    pieces = [(i, i, 0, 0, rows) for i in range(4)]
    pieces += [(4, 4, 0, 0, half), (4, 5, half, half, rows)]
    pieces += [(5, 5, 0, 0, half), (5, 6, half, half, rows)]
    pieces += [(6, 6, 0, 0, half), (6, 4, half, half, rows)]
    pieces += [(7, 7, 0, 0, cut_a), (7, 8, 0, cut_a, cut_b), (7, 9, 0, cut_b, rows)]
    return arrays, pieces, extra


def relay_inputs(own, both, beside_third):
    rows = own.shape[0]
    half = rows // 2
    half_both = both.shape[0] // 2
    back, ahead, low1, high1 = lax.optimization_barrier(
        (seq_send(own, 1, 0), seq_send(own, -1, 0), dp_send(both, 0, 1), dp_send(both, 0, -1))
    )
    up, down, beside, low2, high2 = lax.optimization_barrier(
        (
            seq_send(back[:half], 1, 0),
            seq_send(ahead[half:], -1, 0),
            seq_send(own, 0, 1),
            dp_send(low1, 0, 1),
            dp_send(high1, 0, -1),
        )
    )
    back_beside, ahead_beside, far_beside, low3, high3, extra = lax.optimization_barrier(
        (
            seq_send(beside, 1, 0),
            seq_send(beside, -1, 0),
            seq_send(cat(up, down), 0, 1),
            dp_send(low2, 0, 1),
            dp_send(high2, 0, -1),
            beside_third(low2),
        )
    )
    low4, high4 = dp_send(low3[:half_both], 0, 1), dp_send(high3[half_both:], 0, -1)
    arrays = [own, back, ahead, beside, up, down, ahead_beside, back_beside, far_beside]
    pieces = [(i, i, 0, 0, rows) for i in range(4)]
    pieces += [(4, 4, 0, 0, half), (4, 5, 0, half, rows)]
    pieces += [(i, i + 1, 0, 0, rows) for i in (5, 6, 7)]
    return arrays, pieces, [both, low1, high1, low2, high2, low3, high3, low4, high4], (low1, low2, low3), extra


def hint_kernel(rows, depth, pieces, where_ref, *refs):
    count = len(refs) - 5
    weight_refs, arrays = refs[:9], refs[9:count]
    send_ref, keep_ref, ctx, wgt, sem = refs[count:]
    half_rows = rows // 2
    copies = []

    def copy(src, dst):
        c = pltpu.make_async_copy(src, dst, sem.at[len(copies)])
        c.start()
        copies.append(c)

    for i, block in enumerate(weight_refs[:7]):
        z = where_ref[8 + i]
        for h in range(NH):
            copy(
                block.at[pl.ds(h * depth, depth)],
                wgt.at[pl.ds(pl.multiple_of((h * NZ + z) * depth, 16), depth)],
            )
    z = where_ref[15]
    for h in range(NH):
        copy(weight_refs[7 + h], wgt.at[pl.ds(pl.multiple_of((h * NZ + z) * depth, 16), depth)])
    for block, array, first, lo, hi in pieces:
        for h in range(2):
            top, end = max(lo, h * half_rows), min(hi, (h + 1) * half_rows)
            if top < end:
                at = (h * NS + where_ref[block]) * half_rows + top - h * half_rows
                copy(
                    arrays[array].at[pl.ds(first + top - lo, end - top)],
                    ctx.at[pl.ds(pl.multiple_of(at, 16), end - top)],
                )
    for c in copies:
        c.wait()
    mine = where_ref[16]
    span = NS * half_rows
    step = span // 2

    def body(i, _):
        for out, half in ((send_ref, 1 - mine), (keep_ref, mine)):
            at = pl.multiple_of(half * span + i * step, 16)
            out[pl.ds(pl.multiple_of(i * step, 8), step), :] = jnp.dot(
                ctx[pl.ds(at, step), :], wgt[...], preferred_element_type=F32
            )
        return 0

    lax.fori_loop(0, 2, body, 0)


def hint_matmul(where, arrays, pieces, weights):
    rows, features = arrays[0].shape
    columns = weights[0].shape[1]
    depth = weights[0].shape[0] // 2
    half = NS * rows // 2
    operands = [*weights, *arrays]
    return pl.pallas_call(
        functools.partial(hint_kernel, rows, depth, pieces),
        out_shape=[jax.ShapeDtypeStruct((half, columns), F32)] * 2,
        in_specs=[pl.BlockSpec(memory_space=pltpu.SMEM)] + [pl.BlockSpec(memory_space=pl.ANY)] * len(operands),
        out_specs=[pl.BlockSpec(memory_space=pltpu.VMEM)] * 2,
        scratch_shapes=[
            pltpu.VMEM((2 * half, features), BF16),
            pltpu.VMEM((features, columns), BF16),
            pltpu.SemaphoreType.DMA((40,)),
        ],
        compiler_params=pltpu.CompilerParams(vmem_limit_bytes=24 * 1024 * 1024),
        cost_estimate=pl.CostEstimate(
            flops=2 * 2 * half * features * columns,
            bytes_accessed=2 * (2 * half + columns) * features + 8 * half * columns,
            transcendentals=0,
        ),
        name="hint_matmul",
    )(where, *operands)


def mix_kernel(keep_ref, got_ref, main_ref, bias_ref, mixed_ref, stats_ref):
    rows, columns = keep_ref.shape
    hint = (keep_ref[...] + got_ref[...] + bias_ref[...]).astype(BF16)
    mixed = (main_ref[...].astype(F32) + hint.astype(F32)).astype(BF16)
    mixed_ref[...] = mixed
    values = mixed.astype(F32)
    average = jnp.mean(values, axis=-1, keepdims=True)
    centered = values - average
    spread = jnp.sum(centered * centered, axis=-1, keepdims=True)
    lane = lax.broadcasted_iota(jnp.int32, (rows, 128), 1)
    both = jnp.where(lane == 0, average, spread)
    stats_ref[...] = both.T[0:8, :]


def mix(keep, got, main_cols, bias):
    rows, columns = keep.shape
    return pl.pallas_call(
        mix_kernel,
        out_shape=[
            jax.ShapeDtypeStruct((rows, columns), BF16),
            jax.ShapeDtypeStruct((8, rows), F32),
        ],
        compiler_params=pltpu.CompilerParams(vmem_limit_bytes=16 * 1024 * 1024),
        cost_estimate=pl.CostEstimate(flops=10 * rows * columns, bytes_accessed=12 * rows * columns, transcendentals=0),
        name="mix",
    )(keep, got, main_cols, bias)


def project_kernel(rows, width, pieces, where_ref, *refs):
    count = len(refs) - 14
    arrays = refs[:count]
    own_w, other_w, norm_ref, mod_ref, keep_ref, send_ref, next_ref = refs[count : count + 7]
    xs, normed, w_own, w_other, cols, sem_x, sem_w = refs[count + 7 :]
    deep = width // 2

    x_copies = [[] for _ in range(NS)]
    for k, (block, array, first, lo, hi) in enumerate(pieces):
        x_copies[block].append(
            pltpu.make_async_copy(
                arrays[array].at[pl.ds(first, hi - lo)], xs.at[block, pl.ds(lo, hi - lo)], sem_x.at[k]
            )
        )

    def w_copies(i):
        s = where_ref[i]
        z, h = (2 * s) % NZ, (2 * s) // NZ
        out = []
        for j in range(2):
            src = pl.ds(pl.multiple_of(h * deep, 16), deep)
            dst = pl.ds(j * deep, deep)
            out.append(pltpu.make_async_copy(own_w.at[z + j, src], w_own.at[i, dst], sem_w.at[i, j]))
            out.append(pltpu.make_async_copy(other_w.at[z + j, src], w_other.at[i, dst], sem_w.at[i, 2 + j]))
        return out

    for i in range(NS):
        for c in x_copies[i] + w_copies(i):
            c.start()
    cols[...] = jnp.broadcast_to(norm_ref[0:1, :], (128, rows)).T
    mean_cols = cols[:, 0:1]
    cols[...] = jnp.broadcast_to(norm_ref[1:2, :], (128, rows)).T
    rstd_cols = cols[:, 0:1]
    me = where_ref[17]
    half_tokens = rows // NS
    for i in range(NS):
        s = where_ref[i]
        for c in x_copies[i] + w_copies(i):
            c.wait()
        shift = mod_ref[s, 0:1, :]
        scale = 1.0 + mod_ref[s, 1:2, :]
        values = xs[i].astype(F32)
        normed[i % 2] = ((values - mean_cols) * rstd_cols * scale + shift).astype(BF16)
        rows_next = xs[i, pl.ds(pl.multiple_of(me * half_tokens, 16), half_tokens), :]
        next_ref[s // NY, :, pl.ds(pl.multiple_of((s % NY) * width, 128), width)] = rows_next
        own = jnp.dot(normed[i % 2], w_own[i], preferred_element_type=F32)
        other = jnp.dot(normed[i % 2], w_other[i], preferred_element_type=F32)
        if i == 0:
            keep_ref[...] = own
            send_ref[...] = other
        else:
            keep_ref[...] += own
            send_ref[...] += other


def project(where, arrays, pieces, own_w, other_w, norm_rows, mod):
    rows, width = arrays[0].shape
    columns = own_w.shape[2]
    operands = [*arrays, own_w, other_w]
    half_tokens = rows // NS
    return pl.pallas_call(
        functools.partial(project_kernel, rows, width, pieces),
        out_shape=[
            jax.ShapeDtypeStruct((rows, columns), F32),
            jax.ShapeDtypeStruct((rows, columns), F32),
            jax.ShapeDtypeStruct((2, half_tokens, NY * width), BF16),
        ],
        in_specs=[pl.BlockSpec(memory_space=pltpu.SMEM)]
        + [pl.BlockSpec(memory_space=pl.ANY)] * len(operands)
        + [pl.BlockSpec(memory_space=pltpu.VMEM)] * 2,
        out_specs=[pl.BlockSpec(memory_space=pltpu.VMEM)] * 3,
        scratch_shapes=[
            pltpu.VMEM((NS, rows, width), BF16),
            pltpu.VMEM((2, rows, width), BF16),
            pltpu.VMEM((NS, width, columns), BF16),
            pltpu.VMEM((NS, width, columns), BF16),
            pltpu.VMEM((rows, 128), F32),
            pltpu.SemaphoreType.DMA((len(pieces),)),
            pltpu.SemaphoreType.DMA((NS, 4)),
        ],
        compiler_params=pltpu.CompilerParams(vmem_limit_bytes=36 * 1024 * 1024),
        cost_estimate=pl.CostEstimate(
            flops=4 * rows * NS * width * columns,
            bytes_accessed=2 * NS * width * (rows + 2 * columns) + 8 * rows * columns,
            transcendentals=0,
        ),
        name="project",
    )(where, *operands, norm_rows, mod)


def squares_kernel(keep_ref, got_ref, bias_ref, out_ref):
    rows = keep_ref.shape[0]
    lane = lax.broadcasted_iota(jnp.int32, (rows, 128), 1)
    sums = []
    for ref in (keep_ref, got_ref):
        values = ref[...] + bias_ref[...]
        sums.append(jnp.sum(values * values, axis=-1, keepdims=True))
    out_ref[...] = jnp.where(lane == 0, sums[0], sums[1]).T[0:8, :]


def squares(keep, got, bias):
    rows, columns = keep.shape
    return pl.pallas_call(
        squares_kernel,
        out_shape=jax.ShapeDtypeStruct((8, rows), F32),
        compiler_params=pltpu.CompilerParams(vmem_limit_bytes=12 * 1024 * 1024),
        cost_estimate=pl.CostEstimate(flops=6 * rows * columns, bytes_accessed=8 * rows * columns, transcendentals=0),
        name="squares",
    )(keep, got, bias)


def rotate_kernel(where_ref, keep_ref, got_ref, inv_ref, bias_ref, gain_ref, cos_ref, sin_ref, out_ref, inv):
    rows, columns = keep_ref.shape
    part = rows // NS
    mine = where_ref[16]
    for h in range(2):
        inv[h] = jnp.broadcast_to(inv_ref[h : h + 1, :], (128, rows)).T
    even = lax.broadcasted_iota(jnp.int32, (part, HEAD), 1) % 2 == 0

    def body(s, _):
        for h, ref in enumerate((keep_ref, got_ref)):
            half = mine if h == 0 else 1 - mine
            src = pl.ds(pl.multiple_of(s * part, 16), part)
            dst = pl.ds(pl.multiple_of((2 * s + half) * part, 16), part)
            cosine = cos_ref[dst, :]
            sine = sin_ref[dst, :]
            root = inv[h, src, :]
            for a in range(columns // HEAD):
                lanes = slice(a * HEAD, (a + 1) * HEAD)
                value = (ref[src, lanes] + bias_ref[:, lanes]) * root * gain_ref[:, lanes]
                partner = jnp.where(even, pltpu.roll(value, HEAD - 1, 1), pltpu.roll(value, 1, 1))
                out_ref[dst, lanes] = (value * cosine + partner * sine).astype(BF16)
        return 0

    lax.fori_loop(0, NS, body, 0)


def rotate(where, keep, got, inv_rows, bias, gain, cosine, sine):
    rows, columns = keep.shape
    return pl.pallas_call(
        rotate_kernel,
        out_shape=jax.ShapeDtypeStruct((2 * rows, columns), BF16),
        in_specs=[pl.BlockSpec(memory_space=pltpu.SMEM)] + [pl.BlockSpec(memory_space=pltpu.VMEM)] * 7,
        out_specs=pl.BlockSpec(memory_space=pltpu.VMEM),
        scratch_shapes=[pltpu.VMEM((2, rows, HEAD), F32)],
        compiler_params=pltpu.CompilerParams(vmem_limit_bytes=16 * 1024 * 1024),
        cost_estimate=pl.CostEstimate(flops=20 * rows * columns, bytes_accessed=14 * rows * columns, transcendentals=0),
        name="rotate",
    )(where, keep, got, inv_rows, bias, gain, cosine, sine)


def rope_tables(cell_ids):
    half_head = HEAD // 2
    sixth_head = HEAD // 6
    frame_pairs = half_head - 2 * sixth_head
    lane = jnp.arange(HEAD, dtype=jnp.int32)
    pair_index = lane // 2
    in_frame = pair_index < frame_pairs
    in_height = jnp.logical_and(pair_index >= frame_pairs, pair_index < frame_pairs + sixth_head)
    local_index = jnp.where(
        in_frame,
        pair_index,
        jnp.where(in_height, pair_index - frame_pairs, pair_index - frame_pairs - sixth_head),
    )
    section = jnp.where(in_frame, frame_pairs, sixth_head)
    frequency = jnp.power(10000.0, -local_index.astype(F32) / section.astype(F32))
    frame_ids = cell_ids // (TILE_H * TILE_W)
    row_ids = cell_ids // TILE_W % TILE_H
    col_ids = cell_ids % TILE_W
    position = jnp.where(
        in_frame[None, :],
        frame_ids[:, None],
        jnp.where(in_height[None, :], row_ids[:, None], col_ids[:, None]),
    )
    angles = position.astype(F32) * frequency[None, :]
    sign = jnp.where(lane % 2 == 0, -1.0, 1.0)
    return jnp.cos(angles), jnp.sin(angles) * sign[None, :]


def on_device(
    context,
    main_stream,
    cell_order,
    modulation,
    hint_weight,
    hint_bias,
    weights,
    biases,
    norm_gains,
):
    branch = lax.axis_index("branch")
    seq = lax.axis_index("seq")
    dp = lax.axis_index("dp")
    y, x = seq // NX, seq % NX
    hh, z = dp // NZ, dp % NZ
    where = jnp.stack(
        [((y + dy) % NY) * NX + (x + dx) % NX for dy, dx in REL]
        + [(z + dz) % NZ for dz in (0, -1, 1, -2, 2, -3, 3, 4)]
        + [branch, seq]
    ).astype(jnp.int32)

    tokens, features = main_stream.shape[1:]
    width = features // NS
    part = tokens // 2

    def in_order(own, got):
        return jnp.where(hh == 0, jnp.concatenate([own, got], 0), jnp.concatenate([got, own], 0))

    def send_main(step):
        half = lax.dynamic_slice_in_dim(main_stream[0], branch * part, part, 0)
        half = after(jnp.transpose(half.reshape(part, NS, width), (1, 0, 2)), step)
        return lax.all_to_all(half, "seq", split_axis=0, concat_axis=0, tiled=True).reshape(NS * part, width)

    hint_got = dp_send(hint_weight, 1, 0)
    slot_got = dp_send(after(weights[0], hint_got), 1, 0)
    arrays, pieces, hint_blocks, steps, main_cols = relay_inputs(
        context[0], in_order(hint_weight, hint_got), send_main
    )

    slot_both = after(in_order(weights[0], slot_got), steps[SC_AFTER])
    own_w = lax.all_gather(slot_both, "dp", axis=0, axis_index_groups=Z_GROUPS)

    sent, kept = hint_matmul(where, arrays, pieces, hint_blocks)
    got = core_swap(sent)
    mixed, stats = mix(kept, got, main_cols, hint_bias[None, :])

    rows = NS * part
    lines = rows // 128

    def send_small():
        small = cat(
            stats[0:2].reshape(-1, 128), cell_order.astype(F32).reshape(-1, 128), jnp.zeros((7, 128), F32)
        )
        small = jnp.broadcast_to(small[None], (NS, *small.shape))
        return lax.all_to_all(small, "seq", split_axis=0, concat_axis=0, tiled=True)

    def use_small(small):
        means = small[:, 0:lines].reshape(NS, rows)
        spreads = small[:, lines : 2 * lines].reshape(NS, rows)
        average = jnp.mean(means, axis=0)
        apart = means - average[None, :]
        variance = (jnp.sum(spreads, axis=0) + width * jnp.sum(apart * apart, axis=0)) / features
        norm_rows = cat(average[None], lax.rsqrt(variance + norm_eps)[None], jnp.zeros((6, rows), F32))
        cells = small[:, 2 * lines].reshape(NS * tokens).astype(jnp.int32)
        mod = jnp.transpose(modulation[0].reshape(2, NS, width), (1, 0, 2))
        return norm_rows, mod, *rope_tables(cells)

    arrays, pieces, (norm_rows, mod, cosine, sine) = relay_mixed(mixed, send_small, use_small)
    other_w = core_swap(after(own_w, arrays[4]))
    proj_kept, proj_sent, next_half = project(where, arrays, pieces, own_w, other_w, norm_rows, mod)
    proj_got = core_swap(proj_sent)
    square_rows = squares(proj_kept, proj_got, biases)
    square_tile = square_rows[0:2].reshape(-1, 128)
    all_squares = lax.all_to_all(
        jnp.broadcast_to(square_tile[None], (NS, *square_tile.shape)), "seq", split_axis=0, concat_axis=0, tiled=True
    )
    inv_rms = lax.rsqrt(jnp.sum(all_squares, axis=0) / features + norm_eps).reshape(2, rows)
    rotated = rotate(where, proj_kept, proj_got, inv_rms, biases, norm_gains, cosine, sine)

    next_mine = lax.dynamic_index_in_dim(next_half, branch, 0, keepdims=False)
    next_sent = lax.dynamic_index_in_dim(next_half, 1 - branch, 0, keepdims=False)
    next_got = core_swap(next_sent)
    main_next = jnp.where(
        branch == 0,
        jnp.concatenate([next_mine, next_got], 0),
        jnp.concatenate([next_got, next_mine], 0),
    )
    return (rotated[None, None], main_next[None])


def solution(mesh):
    placed = (
        P("dp", "seq", "branch"),
        P("dp", "seq", None),
        P("dp", "seq"),
        P("dp", None, None),
        P(("branch", "dp"), "seq"),
        P("seq"),
        P("branch", "dp", "seq"),
        P("branch", "seq"),
        P("branch", "seq"),
    )
    return jax.shard_map(
        on_device,
        mesh=mesh,
        in_specs=placed,
        out_specs=(P("branch", "dp", None, "seq"), P("dp", "seq", "branch")),
        check_vma=False,
    )
```

```python
import functools

import jax
import jax.numpy as jnp
from jax import lax
from jax.experimental import pallas as pl
from jax.experimental.pallas import tpu as pltpu
from jax.sharding import PartitionSpec as P

HEAD = 128
TILE_H = 8
TILE_W = 16
norm_eps = 1e-06

F32 = jnp.float32
BF16 = jnp.bfloat16

NY, NX, NH, NZ = 4, 2, 2, 8
NS = NY * NX
SWAP = [(0, 1), (1, 0)]
REL = [(0, 0), (-1, 0), (1, 0), (0, 1), (2, 0), (1, 1), (-1, 1), (2, 1)]
Z_GROUPS = [[hh * NZ + z for z in range(NZ)] for hh in range(NH)]
MIB = 1024 * 1024

HBM = pl.BlockSpec(memory_space=pltpu.HBM)
WHOLE = pl.BlockSpec(memory_space=pltpu.VMEM)
SMALL = pl.CostEstimate(flops=1, bytes_accessed=1, transcendentals=0)
SCALARS = pl.BlockSpec(memory_space=pltpu.SMEM)


def seq_pairs(dy, dx):
    return [(s, ((s // NX + dy) % NY) * NX + (s % NX ^ dx)) for s in range(NS)]


def dp_pairs(dh, dz):
    return [(d, (d // NZ ^ dh) * NZ + (d % NZ + dz) % NZ) for d in range(NH * NZ)]


def seq_send(x, dy, dx):
    return lax.ppermute(x, "seq", seq_pairs(dy, dx))


def dp_send(x, dh, dz):
    return lax.ppermute(x, "dp", dp_pairs(dh, dz))


def core_swap(x):
    return lax.ppermute(x, "branch", SWAP)


def thirds(rows):
    unit = rows // NS
    return 3 * unit, 5 * unit


def after(value, *earlier):
    return lax.optimization_barrier((value, earlier))[0]


def cat(*parts):
    return jnp.concatenate(parts, 0)


def join_kernel(a_ref, b_ref, out_ref):
    half = a_ref.shape[0]
    out_ref[:half, :] = a_ref[...]
    out_ref[half:, :] = b_ref[...]


def join(a, b):
    return pl.pallas_call(
        join_kernel,
        out_shape=jax.ShapeDtypeStruct((2 * a.shape[0], a.shape[1]), a.dtype),
        in_specs=[WHOLE] * 2,
        out_specs=WHOLE,
        cost_estimate=SMALL,
        name="join",
    )(a, b)


def relay_context(own, beside_first, beside_second, beside_third):
    half = own.shape[0] // 2
    back, ahead, extra = lax.optimization_barrier(
        (seq_send(own, 1, 0), seq_send(own, -1, 0), beside_first)
    )
    up, down, beside, more = lax.optimization_barrier(
        (
            seq_send(back[:half], 1, 0),
            seq_send(ahead[half:], -1, 0),
            seq_send(after(own, back), 0, 1),
            beside_second(extra),
        )
    )
    far = join(up, down)
    ahead_beside, back_beside, far_beside, extra = lax.optimization_barrier(
        (seq_send(beside, -1, 0), seq_send(beside, 1, 0), seq_send(far, 0, 1), beside_third(beside))
    )
    return [own, back, ahead, beside, far, ahead_beside, back_beside, far_beside], more, extra


def hint_kernel(rows, where_ref, weight_ref, *refs):
    blocks = refs[:NS]
    other_ref, mine_ref, ctx, wgt, sem = refs[NS:]
    half_rows = rows // 2
    depth = weight_ref.shape[1] // NH
    mine = where_ref[8]
    copies = []

    def copy(src, dst):
        c = pltpu.make_async_copy(src, dst, sem.at[len(copies)])
        c.start()
        copies.append(c)

    def tokens(half, slot):
        for i, block in enumerate(blocks):
            src = pl.ds(pl.multiple_of(half * half_rows, 16), half_rows)
            copy(block.at[src], ctx.at[slot, pl.ds(pl.multiple_of(where_ref[i] * half_rows, 16), half_rows)])

    tokens(1 - mine, 0)
    for h in range(NH):
        for z in range(NZ):
            copy(weight_ref.at[z, pl.ds(h * depth, depth)], wgt.at[pl.ds((h * NZ + z) * depth, depth)])
    tokens(mine, 1)
    for c in copies[: NS + NH * NZ]:
        c.wait()
    other_ref[...] = jnp.dot(ctx[0], wgt[...], preferred_element_type=F32)
    for c in copies[NS + NH * NZ :]:
        c.wait()
    mine_ref[...] = jnp.dot(ctx[1], wgt[...], preferred_element_type=F32)


def hint_matmul(where, blocks, weight):
    rows, features = blocks[0].shape
    columns = weight.shape[2]
    half = NS * rows // 2
    return pl.pallas_call(
        functools.partial(hint_kernel, rows),
        out_shape=[jax.ShapeDtypeStruct((half, columns), F32)] * 2,
        in_specs=[SCALARS] + [HBM] * (1 + NS),
        out_specs=[WHOLE] * 2,
        scratch_shapes=[
            pltpu.VMEM((2, half, features), BF16),
            pltpu.VMEM((features, columns), BF16),
            pltpu.SemaphoreType.DMA((2 * NS + NH * NZ,)),
        ],
        compiler_params=pltpu.CompilerParams(vmem_limit_bytes=60 * MIB),
        cost_estimate=SMALL,
        name="hint",
    )(where, weight, *blocks)


def mix_kernel(keep_ref, got_ref, main_ref, bias_ref, cell_ref, mixed_ref, small_ref):
    rows = keep_ref.shape[0]
    lines = rows // 128
    hint = (keep_ref[...] + got_ref[...] + bias_ref[...]).astype(BF16)
    mixed = (main_ref[...].astype(F32) + hint.astype(F32)).astype(BF16)
    mixed_ref[...] = mixed
    values = mixed.astype(F32)
    average = jnp.mean(values, axis=-1, keepdims=True)
    centered = values - average
    spread = jnp.sum(centered * centered, axis=-1, keepdims=True)
    lane = lax.broadcasted_iota(jnp.int32, (rows, 128), 1)
    both = jnp.where(lane == 0, average, spread).T
    cells = jnp.broadcast_to(cell_ref[...].astype(F32), (8, 128))
    for d in range(NS):
        for r in range(2):
            for k in range(lines):
                small_ref[d, r * lines + k : r * lines + k + 1, :] = both[r : r + 1, k * 128 : (k + 1) * 128]
        small_ref[d, 2 * lines :, :] = cells


def mix(keep, got, main_cols, bias, cells):
    rows, columns = keep.shape
    return pl.pallas_call(
        mix_kernel,
        out_shape=[
            jax.ShapeDtypeStruct((rows, columns), BF16),
            jax.ShapeDtypeStruct((NS, 2 * rows // 128 + 8, 128), F32),
        ],
        compiler_params=pltpu.CompilerParams(vmem_limit_bytes=16 * MIB),
        cost_estimate=SMALL,
        name="mix",
    )(keep, got, main_cols, bias, cells)


def norm_kernel(rows, width, order, pieces, where_ref, norm_ref, mod_ref, *refs):
    mean, rstd, xs, sem = refs[-4:]
    normed_ref, next_ref = refs[-6:-4]
    arrays = refs[:-6]
    copies = []
    for k, (block, array, first, lo, hi) in enumerate(pieces):
        src, dst = arrays[array].at[pl.ds(first, hi - lo)], xs.at[order.index(block), pl.ds(lo, hi - lo)]
        c = pltpu.make_async_copy(src, dst, sem.at[k])
        c.start()
        copies.append(c)
    mean[...] = jnp.broadcast_to(norm_ref[0:1, :], (128, rows)).T
    rstd[...] = jnp.broadcast_to(norm_ref[1:2, :], (128, rows)).T
    for c in copies:
        c.wait()
    step = 128
    tokens = rows // NS
    me = pl.ds(pl.multiple_of(where_ref[9] * tokens, 16), tokens)
    for j, block in enumerate(order):
        s = where_ref[block]
        shift, scale = mod_ref[s, 0:1, :], 1.0 + mod_ref[s, 1:2, :]

        def body(i, _, j=j, shift=shift, scale=scale):
            at = pl.ds(pl.multiple_of(i * step, 16), step)
            into = pl.ds(pl.multiple_of(j * rows + i * step, 16), step)
            average, root = mean[at, :], rstd[at, :]
            for a in range(width // 128):
                lanes = slice(a * 128, (a + 1) * 128)
                values = (xs[j, at, lanes].astype(F32) - average) * root
                normed_ref[into, lanes] = (values * scale[:, lanes] + shift[:, lanes]).astype(BF16)
            return 0

        lax.fori_loop(0, rows // step, body, 0)
        next_ref[j] = xs[j, me, :]


def norm(where, norm_rows, mod, arrays, pieces):
    order = sorted({piece[0] for piece in pieces})
    rows, width = norm_rows.shape[1], mod.shape[2]
    tokens = rows // NS
    return pl.pallas_call(
        functools.partial(norm_kernel, rows, width, order, pieces),
        out_shape=[
            jax.ShapeDtypeStruct((len(order) * rows, width), BF16),
            jax.ShapeDtypeStruct((len(order), tokens, width), BF16),
        ],
        in_specs=[SCALARS, WHOLE, WHOLE] + [HBM] * len(arrays),
        out_specs=[WHOLE] * 2,
        scratch_shapes=[
            pltpu.VMEM((rows, 128), F32),
            pltpu.VMEM((rows, 128), F32),
            pltpu.VMEM((len(order), rows, width), BF16),
            pltpu.SemaphoreType.DMA((len(pieces),)),
        ],
        compiler_params=pltpu.CompilerParams(vmem_limit_bytes=60 * MIB),
        cost_estimate=SMALL,
        name="norm",
    )(where, norm_rows, mod, *arrays)


def next_kernel(where_ref, first_ref, second_ref, *refs):
    pieces, out_ref, whole = refs[:-2], refs[-2], refs[-1]
    tokens, width = first_ref.shape[1:]

    def put(block, part):
        s = where_ref[block]
        out_ref[s // NY, :, pl.ds(pl.multiple_of((s % NY) * width, 128), width)] = part

    count = first_ref.shape[0]
    for j in range(count):
        put(j, first_ref[j])
    for j in range(second_ref.shape[0]):
        put(count + j, second_ref[j])
    at = 0
    for ref in pieces:
        whole[at : at + ref.shape[0], :] = ref[...]
        at += ref.shape[0]
    put(NS - 1, whole[pl.ds(pl.multiple_of(where_ref[9] * tokens, 16), tokens), :])


def next_rows(where, first, second, last):
    tokens, width = first.shape[1:]
    return pl.pallas_call(
        next_kernel,
        out_shape=jax.ShapeDtypeStruct((2, tokens, NY * width), BF16),
        in_specs=[SCALARS] + [WHOLE] * (2 + len(last)),
        out_specs=WHOLE,
        scratch_shapes=[pltpu.VMEM((sum(piece.shape[0] for piece in last), width), BF16)],
        compiler_params=pltpu.CompilerParams(vmem_limit_bytes=16 * MIB),
        cost_estimate=SMALL,
        name="next_rows",
    )(where, first, second, *last)


def project_kernel(counts, cuts, where_ref, *refs):
    sets = len(counts) + len(cuts) - 2
    mine, other = refs[:sets], refs[sets : 2 * sets]
    w_ref, bias_ref, norm_ref, norm_other_ref, mod_ref, out_ref, squares_ref = refs[2 * sets : 2 * sets + 7]
    xs, wgt, raw, mean, rstd, sem_x, sem_w = refs[2 * sets + 7 :]
    rows = out_ref.shape[0] // 2
    width = wgt.shape[0] // NS
    deep = width // 2
    copies = []
    i = 0
    for count, a, b in zip(counts, mine, other):
        for j in range(count):
            src, lanes = pl.ds(j * rows, rows), pl.ds(i * width, width)
            s = where_ref[i]
            z, h = lax.rem(2 * s, NZ), lax.div(2 * s, NZ)
            from_w = pl.ds(pl.multiple_of(h * deep, 16), deep)
            copies.append(
                [
                    pltpu.make_async_copy(w_ref.at[z, from_w], wgt.at[pl.ds(i * width, deep)], sem_w.at[i, 0]),
                    pltpu.make_async_copy(
                        w_ref.at[z + 1, from_w], wgt.at[pl.ds(i * width + deep, deep)], sem_w.at[i, 1]
                    ),
                ]
            )
            if i < NS - 1:
                copies[i] += [
                    pltpu.make_async_copy(a.at[src], xs.at[pl.ds(0, rows), lanes], sem_x.at[2 * i]),
                    pltpu.make_async_copy(b.at[src], xs.at[pl.ds(rows, rows), lanes], sem_x.at[2 * i + 1]),
                ]
            i += 1
    raw_copies = [
        pltpu.make_async_copy(
            refs[side * sets + len(counts) - 1 + k],
            raw.at[pl.ds(side * rows + cuts[k], cuts[k + 1] - cuts[k])],
            sem_x.at[2 * NS + side * (len(cuts) - 1) + k],
        )
        for side in range(2)
        for k in range(len(cuts) - 1)
    ]

    def start(i):
        for c in copies[i] + copies[i + 1]:
            c.start()

    start(0)
    for c in raw_copies:
        c.start()
    start(2)
    for part, ref in enumerate((norm_ref, norm_other_ref)):
        at = pl.ds(part * rows, rows)
        mean[at, :] = jnp.broadcast_to(ref[0:1, :], (128, rows)).T
        rstd[at, :] = jnp.broadcast_to(ref[1:2, :], (128, rows)).T
    s = where_ref[NS - 1]
    shift, scale = mod_ref[s, 0:1, :], 1.0 + mod_ref[s, 1:2, :]
    for i in range(0, NS, 2):
        for c in copies[i] + copies[i + 1]:
            c.wait()
        if i + 4 < NS:
            start(i + 4)
        if i == NS - 2:
            for c in raw_copies:
                c.wait()
            for a in range(width // 128):
                lanes = slice(a * 128, (a + 1) * 128)
                values = (raw[:, lanes].astype(F32) - mean[...]) * rstd[...]
                xs[:, (NS - 1) * width + a * 128 : (NS - 1) * width + (a + 1) * 128] = (
                    values * scale[:, lanes] + shift[:, lanes]
                ).astype(BF16)
        deep_lanes = pl.ds(i * width, 2 * width)
        for part in range(2):
            at = pl.ds(part * rows, rows)
            product = jnp.dot(xs[at, deep_lanes], wgt[deep_lanes, :], preferred_element_type=F32)
            if i == 0:
                out_ref[at, :] = product + bias_ref[...]
            else:
                out_ref[at, :] += product
    lane = lax.broadcasted_iota(jnp.int32, (rows, 128), 1)
    sums = []
    for part in range(2):
        values = out_ref[pl.ds(part * rows, rows), :]
        sums.append(jnp.sum(values * values, axis=-1, keepdims=True))
    both = jnp.where(lane == 0, sums[0], sums[1]).T
    lines = rows // 128
    for d in range(NS):
        for r in range(2):
            for k in range(lines):
                squares_ref[d, r * lines + k : r * lines + k + 1, :] = both[r : r + 1, k * 128 : (k + 1) * 128]


def project(where, mine, other, weight, bias, norm_rows, norm_other, mod):
    width, columns = mine[0].shape[1], weight.shape[2]
    counts = [4, 3, 1]
    rows = mine[0].shape[0] // counts[0]
    cuts = [0, *thirds(rows), rows]
    operands = [*mine, *other, weight]
    return pl.pallas_call(
        functools.partial(project_kernel, counts, cuts),
        out_shape=[
            jax.ShapeDtypeStruct((2 * rows, columns), F32),
            jax.ShapeDtypeStruct((NS, 2 * rows // 128, 128), F32),
        ],
        in_specs=[SCALARS] + [HBM] * len(operands) + [WHOLE] * 4,
        out_specs=[WHOLE] * 2,
        scratch_shapes=[
            pltpu.VMEM((2 * rows, NS * width), BF16),
            pltpu.VMEM((NS * width, columns), BF16),
            pltpu.VMEM((2 * rows, width), BF16),
            pltpu.VMEM((2 * rows, 128), F32),
            pltpu.VMEM((2 * rows, 128), F32),
            pltpu.SemaphoreType.DMA((2 * NS + 2 * len(cuts),)),
            pltpu.SemaphoreType.DMA((NS, 2)),
        ],
        compiler_params=pltpu.CompilerParams(vmem_limit_bytes=60 * MIB),
        cost_estimate=pl.CostEstimate(
            flops=4 * rows * NS * width * columns,
            bytes_accessed=2 * NS * width * (2 * rows + columns) + 8 * rows * columns,
            transcendentals=0,
        ),
        name="project",
    )(where, *operands, bias, norm_rows, norm_other, mod)


def turn_kernel(where_ref, proj_ref, gain_ref, cos_ref, sin_ref, out_ref):
    tokens, columns = out_ref.shape
    part = tokens // 2 // NS
    mine = where_ref[8]
    even = lax.broadcasted_iota(jnp.int32, (part, HEAD), 1) % 2 == 0

    def body(s, _):
        for h in range(2):
            half = mine if h == 0 else 1 - mine
            src = pl.ds(pl.multiple_of((h * NS + s) * part, 16), part)
            dst = pl.ds(pl.multiple_of((2 * s + half) * part, 16), part)
            cosine, sine = cos_ref[dst, :], sin_ref[dst, :]
            for a in range(columns // HEAD):
                lanes = slice(a * HEAD, (a + 1) * HEAD)
                value = proj_ref[src, lanes] * gain_ref[:, lanes]
                partner = jnp.where(even, pltpu.roll(value, HEAD - 1, 1), pltpu.roll(value, 1, 1))
                out_ref[dst, lanes] = value * cosine + partner * sine
        return 0

    lax.fori_loop(0, NS, body, 0)


def turn(where, proj, gain, cosine, sine):
    tokens, columns = proj.shape
    return pl.pallas_call(
        turn_kernel,
        out_shape=jax.ShapeDtypeStruct((tokens, columns), F32),
        in_specs=[SCALARS] + [WHOLE] * 4,
        out_specs=WHOLE,
        compiler_params=pltpu.CompilerParams(vmem_limit_bytes=60 * MIB),
        cost_estimate=pl.CostEstimate(flops=10 * tokens * columns, bytes_accessed=9 * tokens * columns, transcendentals=0),
        name="turn",
    )(where, proj, gain, cosine, sine)


def rope_tables(cell_ids):
    half_head = HEAD // 2
    sixth_head = HEAD // 6
    frame_pairs = half_head - 2 * sixth_head
    lane = jnp.arange(HEAD, dtype=jnp.int32)
    pair_index = lane // 2
    in_frame = pair_index < frame_pairs
    in_height = jnp.logical_and(pair_index >= frame_pairs, pair_index < frame_pairs + sixth_head)
    local_index = jnp.where(
        in_frame,
        pair_index,
        jnp.where(in_height, pair_index - frame_pairs, pair_index - frame_pairs - sixth_head),
    )
    section = jnp.where(in_frame, frame_pairs, sixth_head)
    frequency = jnp.power(10000.0, -local_index.astype(F32) / section.astype(F32))
    frame_ids = cell_ids // (TILE_H * TILE_W)
    row_ids = cell_ids // TILE_W % TILE_H
    col_ids = cell_ids % TILE_W
    position = jnp.where(
        in_frame[None, :],
        frame_ids[:, None],
        jnp.where(in_height[None, :], row_ids[:, None], col_ids[:, None]),
    )
    angles = position.astype(F32) * frequency[None, :]
    sign = jnp.where(lane % 2 == 0, -1.0, 1.0)
    return jnp.cos(angles), jnp.sin(angles) * sign[None, :]


def on_device(
    context,
    main_stream,
    cell_order,
    modulation,
    hint_weight,
    hint_bias,
    weights,
    biases,
    norm_gains,
):
    branch = lax.axis_index("branch")
    seq = lax.axis_index("seq")
    dp = lax.axis_index("dp")
    y, x = seq // NX, seq % NX
    hh = dp // NZ
    where = jnp.stack(
        [((y + dy) % NY) * NX + (x + dx) % NX for dy, dx in REL] + [branch, seq]
    ).astype(jnp.int32)

    tokens, features = main_stream.shape[1:]
    width = features // NS
    part = tokens // 2
    rows = NS * part
    lines = rows // 128

    def both_columns(own, other):
        return jnp.where(hh == 0, cat(own, other), cat(other, own))

    def along_z(both):
        return lax.all_gather(both, "dp", axis=0, axis_index_groups=Z_GROUPS)

    hint_both = both_columns(hint_weight, dp_send(hint_weight, 1, 0))
    hint_weights = along_z(hint_both)
    slot = weights[0]
    slot_other = dp_send(slot, 1, 0)

    def send_main(beside):
        half = lax.dynamic_slice_in_dim(main_stream[0], branch * part, part, 0)
        half = after(jnp.transpose(half.reshape(part, NS, width), (1, 0, 2)), beside)
        return lax.all_to_all(half, "seq", split_axis=0, concat_axis=0, tiled=True).reshape(rows, width)

    blocks, slot_both, main_cols = relay_context(
        context[0], slot_other, lambda slot_other: both_columns(slot, slot_other), send_main
    )
    weight = along_z(slot_both)

    sent, kept = hint_matmul(where, blocks, hint_weights)
    got = core_swap(sent)
    mixed, small = mix(kept, got, main_cols, hint_bias[None, :], cell_order)

    half = rows // 2
    cut_a, cut_b = thirds(rows)
    back, ahead, beside, small = lax.optimization_barrier(
        (
            seq_send(mixed, 1, 0),
            seq_send(mixed, -1, 0),
            seq_send(mixed, 0, 1),
            lax.all_to_all(small, "seq", split_axis=0, concat_axis=0, tiled=True),
        )
    )
    up = seq_send(cat(back[:half], beside[half:]), 1, 0)
    down = seq_send(cat(beside[:half], ahead[half:]), -1, 0)
    over = seq_send(cat(back[:half], ahead[half:]), 0, 1)
    means = small[:, 0:lines].reshape(NS, rows)
    spreads = small[:, lines : 2 * lines].reshape(NS, rows)
    average = jnp.mean(means, axis=0)
    apart = means - average[None, :]
    variance = (jnp.sum(spreads, axis=0) + width * jnp.sum(apart * apart, axis=0)) / features
    norm_rows = cat(average[None], lax.rsqrt(variance + norm_eps)[None], jnp.zeros((6, rows), F32))
    cells = small[:, 2 * lines].reshape(NS * tokens).astype(jnp.int32)
    mod = jnp.transpose(modulation[0].reshape(2, NS, width), (1, 0, 2))
    first, first_next = norm(
        where, norm_rows, mod, [mixed, back, ahead, beside], [(i, i, 0, 0, rows) for i in range(4)]
    )
    up, down, over = lax.optimization_barrier((up, down, over))
    first_got = core_swap(first)
    last = [
        seq_send(up[:cut_a], 0, 1),
        seq_send(cat(over[cut_a:half], up[half:cut_b]), 1, 0),
        seq_send(over[cut_b:], -1, 0),
    ]
    second, second_next = norm(
        where,
        norm_rows,
        mod,
        [up, down, over],
        [
            (4, 0, 0, 0, half),
            (4, 1, half, half, rows),
            (5, 1, 0, 0, half),
            (5, 2, half, half, rows),
            (6, 2, 0, 0, half),
            (6, 0, half, half, rows),
        ],
    )
    tables = rope_tables(after(cells, up))
    norm_other = core_swap(after(norm_rows, up))
    last, second, tables, norm_other = lax.optimization_barrier((last, second, tables, norm_other))
    second_got = core_swap(second)
    last_got = [core_swap(piece) for piece in last]
    next_half = next_rows(where, first_next, second_next, last)

    weight = after(weight, last, next_half)
    proj, squares = project(
        where, [first, second, *last], [first_got, second_got, *last_got], weight, biases, norm_rows, norm_other, mod
    )
    squares = lax.all_to_all(squares, "seq", split_axis=0, concat_axis=0, tiled=True)
    turned = turn(where, proj, norm_gains, *tables)

    next_mine = lax.dynamic_index_in_dim(next_half, branch, 0, keepdims=False)
    next_sent = lax.dynamic_index_in_dim(next_half, 1 - branch, 0, keepdims=False)
    next_got = core_swap(next_sent)
    main_next = jnp.where(branch == 0, cat(next_mine, next_got), cat(next_got, next_mine))

    squares, main_next, turned = lax.optimization_barrier((squares, main_next, turned))
    inv_rms = lax.rsqrt(jnp.sum(squares, axis=0) / features + norm_eps).reshape(2, NS, part)
    inv_rms = jnp.where(branch == 0, inv_rms, inv_rms[::-1])
    inv_rms = jnp.transpose(inv_rms, (1, 0, 2)).reshape(NS * tokens)
    rotated = (turned * inv_rms[:, None]).astype(BF16)
    return (rotated[None, None], main_next[None])


def solution(mesh):
    placed = (
        P("dp", "seq", "branch"),
        P("dp", "seq", None),
        P("dp", "seq"),
        P("dp", None, None),
        P(("branch", "dp"), "seq"),
        P("seq"),
        P("branch", "dp", "seq"),
        P("branch", "seq"),
        P("branch", "seq"),
    )
    return jax.shard_map(
        on_device,
        mesh=mesh,
        in_specs=placed,
        out_specs=(P("branch", "dp", None, "seq"), P("dp", "seq", "branch")),
        check_vma=False,
    )
```

```python
import functools

import jax
import jax.numpy as jnp
from jax import lax
from jax.experimental import pallas as pl
from jax.experimental.pallas import tpu as pltpu
from jax.sharding import PartitionSpec as P

HEAD = 128
TILE_H = 8
TILE_W = 16
norm_eps = 1e-06

F32 = jnp.float32
BF16 = jnp.bfloat16

NY, NX, NH, NZ = 4, 2, 2, 8
NS = NY * NX
SWAP = [(0, 1), (1, 0)]
REL = [(0, 0), (-1, 0), (1, 0), (0, 1), (2, 0), (1, 1), (-1, 1), (2, 1)]
Z_GROUPS = [[hh * NZ + z for z in range(NZ)] for hh in range(NH)]
MIB = 1024 * 1024

HBM = pl.BlockSpec(memory_space=pltpu.HBM)
WHOLE = pl.BlockSpec(memory_space=pltpu.VMEM)
SMALL = pl.CostEstimate(flops=1, bytes_accessed=1, transcendentals=0)
SCALARS = pl.BlockSpec(memory_space=pltpu.SMEM)


def seq_pairs(dy, dx):
    return [(s, ((s // NX + dy) % NY) * NX + (s % NX ^ dx)) for s in range(NS)]


def dp_pairs(dh, dz):
    return [(d, (d // NZ ^ dh) * NZ + (d % NZ + dz) % NZ) for d in range(NH * NZ)]


def seq_send(x, dy, dx):
    return lax.ppermute(x, "seq", seq_pairs(dy, dx))


def dp_send(x, dh, dz):
    return lax.ppermute(x, "dp", dp_pairs(dh, dz))


def core_swap(x):
    return lax.ppermute(x, "branch", SWAP)


def thirds(rows):
    unit = rows // NS
    return 3 * unit, 5 * unit


def after(value, *earlier):
    return lax.optimization_barrier((value, earlier))[0]


def cat(*parts):
    return jnp.concatenate(parts, 0)


def split_kernel(where_ref, main_ref, out_ref):
    tokens, width = out_ref.shape[1:]
    at = pl.ds(pl.multiple_of(where_ref[8] * tokens, 16), tokens)
    for s in range(NS):
        out_ref[s] = main_ref[at, s * width : (s + 1) * width]


def split_columns(where, main):
    tokens, features = main.shape
    return pl.pallas_call(
        split_kernel,
        out_shape=jax.ShapeDtypeStruct((NS, tokens // 2, features // NS), main.dtype),
        in_specs=[SCALARS, WHOLE],
        out_specs=WHOLE,
        compiler_params=pltpu.CompilerParams(vmem_limit_bytes=16 * MIB),
        cost_estimate=SMALL,
        name="split_columns",
    )(where, main)


def relay_context(own, slot_other, join_slot, main_half, where):
    back, ahead, slot_other = lax.optimization_barrier((seq_send(own, 1, 0), seq_send(own, -1, 0), slot_other))
    far, beside, slot_both = lax.optimization_barrier(
        (seq_send(back, 1, 0), seq_send(after(own, back), 0, 1), join_slot(slot_other))
    )
    ahead_beside, back_beside, far_beside, main_half, where = lax.optimization_barrier(
        (seq_send(beside, -1, 0), seq_send(beside, 1, 0), seq_send(far, 0, 1), main_half, where)
    )
    return [own, back, ahead, beside, far, ahead_beside, back_beside, far_beside], slot_both, main_half, where


def hint_kernel(rows, where_ref, weight_ref, *refs):
    blocks = refs[:NS]
    other_ref, mine_ref, ctx, wgt, sem = refs[NS:]
    half_rows = rows // 2
    depth = weight_ref.shape[1] // NH
    mine, column = where_ref[8], where_ref[10]
    copies = []

    def copy(src, dst):
        c = pltpu.make_async_copy(src, dst, sem.at[len(copies)])
        c.start()
        copies.append(c)

    def tokens(half, slot):
        for i, block in enumerate(blocks):
            src = pl.ds(pl.multiple_of(half * half_rows, 16), half_rows)
            copy(block.at[src], ctx.at[slot, pl.ds(pl.multiple_of(where_ref[i] * half_rows, 16), half_rows)])

    def column_rows(col):
        first = jnp.where(col == column, 0, depth)
        for z in range(NZ):
            src = pl.ds(pl.multiple_of(first, 16), depth)
            copy(weight_ref.at[z, src], wgt.at[pl.ds((col * NZ + z) * depth, depth)])

    tokens(1 - mine, 0)
    column_rows(0)
    column_rows(1)
    tokens(mine, 1)
    deep = NZ * depth
    done = 0
    for count, out_ref, slot, k in ((NS + NZ, other_ref, 0, 0), (NZ, other_ref, 0, 1), (NS, mine_ref, 1, None)):
        for c in copies[done : done + count]:
            c.wait()
        done += count
        if k is None:
            out_ref[...] = jnp.dot(ctx[slot], wgt[...], preferred_element_type=F32)
        else:
            lanes = slice(k * deep, (k + 1) * deep)
            product = jnp.dot(ctx[slot, :, lanes], wgt[lanes, :], preferred_element_type=F32)
            out_ref[...] = out_ref[...] + product if k else product


def hint_matmul(where, blocks, weight):
    rows, features = blocks[0].shape
    columns = weight.shape[2]
    half = NS * rows // 2
    return pl.pallas_call(
        functools.partial(hint_kernel, rows),
        out_shape=[jax.ShapeDtypeStruct((half, columns), F32)] * 2,
        in_specs=[SCALARS] + [HBM] * (1 + NS),
        out_specs=[WHOLE] * 2,
        scratch_shapes=[
            pltpu.VMEM((2, half, features), BF16),
            pltpu.VMEM((features, columns), BF16),
            pltpu.SemaphoreType.DMA((2 * NS + NH * NZ,)),
        ],
        compiler_params=pltpu.CompilerParams(vmem_limit_bytes=60 * MIB),
        cost_estimate=SMALL,
        name="hint",
    )(where, weight, *blocks)


def mix_kernel(keep_ref, got_ref, main_ref, bias_ref, cell_ref, mixed_ref, small_ref):
    rows = keep_ref.shape[0]
    lines = rows // 128
    hint = (keep_ref[...] + got_ref[...] + bias_ref[...]).astype(BF16)
    mixed = (main_ref[...].astype(F32) + hint.astype(F32)).astype(BF16)
    mixed_ref[...] = mixed
    values = mixed.astype(F32)
    average = jnp.mean(values, axis=-1, keepdims=True)
    centered = values - average
    spread = jnp.sum(centered * centered, axis=-1, keepdims=True)
    lane = lax.broadcasted_iota(jnp.int32, (rows, 128), 1)
    both = jnp.where(lane == 0, average, spread).T
    cells = jnp.broadcast_to(cell_ref[...].astype(F32), (8, 128))
    for d in range(NS):
        for r in range(2):
            for k in range(lines):
                small_ref[d, r * lines + k : r * lines + k + 1, :] = both[r : r + 1, k * 128 : (k + 1) * 128]
        small_ref[d, 2 * lines :, :] = cells


def mix(keep, got, main_cols, bias, cells):
    rows, columns = keep.shape
    return pl.pallas_call(
        mix_kernel,
        out_shape=[
            jax.ShapeDtypeStruct((rows, columns), BF16),
            jax.ShapeDtypeStruct((NS, 2 * rows // 128 + 8, 128), F32),
        ],
        compiler_params=pltpu.CompilerParams(vmem_limit_bytes=16 * MIB),
        cost_estimate=SMALL,
        name="mix",
    )(keep, got, main_cols, bias, cells)


def norm_kernel(rows, width, order, pieces, where_ref, norm_ref, mod_ref, *refs):
    mean, rstd, xs, sem = refs[-4:]
    normed_ref, next_ref = refs[-6:-4]
    arrays = refs[:-6]
    copies = []
    for k, (block, array, first, lo, hi) in enumerate(pieces):
        src, dst = arrays[array].at[pl.ds(first, hi - lo)], xs.at[order.index(block), pl.ds(lo, hi - lo)]
        c = pltpu.make_async_copy(src, dst, sem.at[k])
        c.start()
        copies.append(c)
    mean[...] = jnp.broadcast_to(norm_ref[0:1, :], (128, rows)).T
    rstd[...] = jnp.broadcast_to(norm_ref[1:2, :], (128, rows)).T
    for c in copies:
        c.wait()
    step = 128
    tokens = rows // NS
    me = pl.ds(pl.multiple_of(where_ref[9] * tokens, 16), tokens)
    for j, block in enumerate(order):
        s = where_ref[block]
        shift, scale = mod_ref[s, 0:1, :], 1.0 + mod_ref[s, 1:2, :]

        def body(i, _, j=j, shift=shift, scale=scale):
            at = pl.ds(pl.multiple_of(i * step, 16), step)
            into = pl.ds(pl.multiple_of(j * rows + i * step, 16), step)
            average, root = mean[at, :], rstd[at, :]
            for a in range(width // 128):
                lanes = slice(a * 128, (a + 1) * 128)
                values = (xs[j, at, lanes].astype(F32) - average) * root
                normed_ref[into, lanes] = (values * scale[:, lanes] + shift[:, lanes]).astype(BF16)
            return 0

        lax.fori_loop(0, rows // step, body, 0)
        next_ref[j] = xs[j, me, :]


def norm(where, norm_rows, mod, arrays, pieces):
    order = sorted({piece[0] for piece in pieces})
    rows, width = norm_rows.shape[1], mod.shape[2]
    tokens = rows // NS
    return pl.pallas_call(
        functools.partial(norm_kernel, rows, width, order, pieces),
        out_shape=[
            jax.ShapeDtypeStruct((len(order) * rows, width), BF16),
            jax.ShapeDtypeStruct((len(order), tokens, width), BF16),
        ],
        in_specs=[SCALARS, WHOLE, WHOLE] + [HBM] * len(arrays),
        out_specs=[WHOLE] * 2,
        scratch_shapes=[
            pltpu.VMEM((rows, 128), F32),
            pltpu.VMEM((rows, 128), F32),
            pltpu.VMEM((len(order), rows, width), BF16),
            pltpu.SemaphoreType.DMA((len(pieces),)),
        ],
        compiler_params=pltpu.CompilerParams(vmem_limit_bytes=60 * MIB),
        cost_estimate=SMALL,
        name="norm",
    )(where, norm_rows, mod, *arrays)


def next_kernel(where_ref, first_ref, second_ref, *refs):
    pieces, out_ref, whole = refs[:-2], refs[-2], refs[-1]
    tokens, width = first_ref.shape[1:]

    def put(block, part):
        s = where_ref[block]
        out_ref[s // NY, :, pl.ds(pl.multiple_of((s % NY) * width, 128), width)] = part

    count = first_ref.shape[0]
    for j in range(count):
        put(j, first_ref[j])
    for j in range(second_ref.shape[0]):
        put(count + j, second_ref[j])
    at = 0
    for ref in pieces:
        whole[at : at + ref.shape[0], :] = ref[...]
        at += ref.shape[0]
    put(NS - 1, whole[pl.ds(pl.multiple_of(where_ref[9] * tokens, 16), tokens), :])


def next_rows(where, first, second, last):
    tokens, width = first.shape[1:]
    return pl.pallas_call(
        next_kernel,
        out_shape=jax.ShapeDtypeStruct((2, tokens, NY * width), BF16),
        in_specs=[SCALARS] + [WHOLE] * (2 + len(last)),
        out_specs=WHOLE,
        scratch_shapes=[pltpu.VMEM((sum(piece.shape[0] for piece in last), width), BF16)],
        compiler_params=pltpu.CompilerParams(vmem_limit_bytes=16 * MIB),
        cost_estimate=SMALL,
        name="next_rows",
    )(where, first, second, *last)


def project_kernel(counts, cuts, where_ref, *refs):
    sets = len(counts) + len(cuts) - 2
    mine, other = refs[:sets], refs[sets : 2 * sets]
    w_ref, bias_ref, norm_ref, norm_other_ref, mod_ref, out_ref, squares_ref = refs[2 * sets : 2 * sets + 7]
    xs, wgt, raw, mean, rstd, sem_x, sem_w = refs[2 * sets + 7 :]
    rows = out_ref.shape[0] // 2
    width = wgt.shape[0] // NS
    deep = width // 2
    copies = []
    i = 0
    for count, a, b in zip(counts, mine, other):
        for j in range(count):
            src, lanes = pl.ds(j * rows, rows), pl.ds(i * width, width)
            s = where_ref[i]
            z, h = lax.rem(2 * s, NZ), lax.div(2 * s, NZ)
            from_w = pl.ds(pl.multiple_of(h * deep, 16), deep)
            copies.append(
                [
                    pltpu.make_async_copy(w_ref.at[z, from_w], wgt.at[pl.ds(i * width, deep)], sem_w.at[i, 0]),
                    pltpu.make_async_copy(
                        w_ref.at[z + 1, from_w], wgt.at[pl.ds(i * width + deep, deep)], sem_w.at[i, 1]
                    ),
                ]
            )
            if i < NS - 1:
                copies[i] += [
                    pltpu.make_async_copy(a.at[src], xs.at[pl.ds(0, rows), lanes], sem_x.at[2 * i]),
                    pltpu.make_async_copy(b.at[src], xs.at[pl.ds(rows, rows), lanes], sem_x.at[2 * i + 1]),
                ]
            i += 1
    raw_copies = [
        pltpu.make_async_copy(
            refs[side * sets + len(counts) - 1 + k],
            raw.at[pl.ds(side * rows + cuts[k], cuts[k + 1] - cuts[k])],
            sem_x.at[2 * NS + side * (len(cuts) - 1) + k],
        )
        for side in range(2)
        for k in range(len(cuts) - 1)
    ]

    def start(i):
        for c in copies[i] + copies[i + 1]:
            c.start()

    start(0)
    for c in raw_copies:
        c.start()
    start(2)
    for part, ref in enumerate((norm_ref, norm_other_ref)):
        at = pl.ds(part * rows, rows)
        mean[at, :] = jnp.broadcast_to(ref[0:1, :], (128, rows)).T
        rstd[at, :] = jnp.broadcast_to(ref[1:2, :], (128, rows)).T
    s = where_ref[NS - 1]
    shift, scale = mod_ref[s, 0:1, :], 1.0 + mod_ref[s, 1:2, :]
    sums = []
    for i in range(0, NS, 2):
        for c in copies[i] + copies[i + 1]:
            c.wait()
        if i + 4 < NS:
            start(i + 4)
        if i == NS - 2:
            for c in raw_copies:
                c.wait()
            for a in range(width // 128):
                lanes = slice(a * 128, (a + 1) * 128)
                values = (raw[:, lanes].astype(F32) - mean[...]) * rstd[...]
                xs[:, (NS - 1) * width + a * 128 : (NS - 1) * width + (a + 1) * 128] = (
                    values * scale[:, lanes] + shift[:, lanes]
                ).astype(BF16)
        deep_lanes = pl.ds(i * width, 2 * width)
        for part in range(2):
            at = pl.ds(part * rows, rows)
            product = jnp.dot(xs[at, deep_lanes], wgt[deep_lanes, :], preferred_element_type=F32)
            if i == 0:
                out_ref[at, :] = product + bias_ref[...]
            elif i < NS - 2:
                out_ref[at, :] += product
            else:
                values = out_ref[at, :] + product
                out_ref[at, :] = values
                sums.append(jnp.sum(values * values, axis=-1, keepdims=True))
    lane = lax.broadcasted_iota(jnp.int32, (rows, 128), 1)
    both = jnp.where(lane == 0, sums[0], sums[1]).T
    lines = rows // 128
    for d in range(NS):
        for r in range(2):
            for k in range(lines):
                squares_ref[d, r * lines + k : r * lines + k + 1, :] = both[r : r + 1, k * 128 : (k + 1) * 128]


def project(where, mine, other, weight, bias, norm_rows, norm_other, mod):
    width, columns = mine[0].shape[1], weight.shape[2]
    counts = [4, 3, 1]
    rows = mine[0].shape[0] // counts[0]
    cuts = [0, *thirds(rows), rows]
    operands = [*mine, *other, weight]
    return pl.pallas_call(
        functools.partial(project_kernel, counts, cuts),
        out_shape=[
            jax.ShapeDtypeStruct((2 * rows, columns), F32),
            jax.ShapeDtypeStruct((NS, 2 * rows // 128, 128), F32),
        ],
        in_specs=[SCALARS] + [HBM] * len(operands) + [WHOLE] * 4,
        out_specs=[WHOLE] * 2,
        scratch_shapes=[
            pltpu.VMEM((2 * rows, NS * width), BF16),
            pltpu.VMEM((NS * width, columns), BF16),
            pltpu.VMEM((2 * rows, width), BF16),
            pltpu.VMEM((2 * rows, 128), F32),
            pltpu.VMEM((2 * rows, 128), F32),
            pltpu.SemaphoreType.DMA((2 * NS + 2 * len(cuts),)),
            pltpu.SemaphoreType.DMA((NS, 2)),
        ],
        compiler_params=pltpu.CompilerParams(vmem_limit_bytes=60 * MIB),
        cost_estimate=pl.CostEstimate(
            flops=4 * rows * NS * width * columns,
            bytes_accessed=2 * NS * width * (2 * rows + columns) + 8 * rows * columns,
            transcendentals=0,
        ),
        name="project",
    )(where, *operands, bias, norm_rows, norm_other, mod)


def turn_kernel(where_ref, proj_ref, gain_ref, cos_ref, sin_ref, out_ref):
    tokens, columns = out_ref.shape
    part = tokens // 2 // NS
    mine = where_ref[8]
    even = lax.broadcasted_iota(jnp.int32, (part, HEAD), 1) % 2 == 0

    def body(s, _):
        for h in range(2):
            half = mine if h == 0 else 1 - mine
            src = pl.ds(pl.multiple_of((h * NS + s) * part, 16), part)
            dst = pl.ds(pl.multiple_of((2 * s + half) * part, 16), part)
            cosine, sine = cos_ref[dst, :], sin_ref[dst, :]
            for a in range(columns // HEAD):
                lanes = slice(a * HEAD, (a + 1) * HEAD)
                value = proj_ref[src, lanes] * gain_ref[:, lanes]
                partner = jnp.where(even, pltpu.roll(value, HEAD - 1, 1), pltpu.roll(value, 1, 1))
                out_ref[dst, lanes] = value * cosine + partner * sine
        return 0

    lax.fori_loop(0, NS, body, 0)


def turn(where, proj, gain, cosine, sine):
    tokens, columns = proj.shape
    return pl.pallas_call(
        turn_kernel,
        out_shape=jax.ShapeDtypeStruct((tokens, columns), F32),
        in_specs=[SCALARS] + [WHOLE] * 4,
        out_specs=WHOLE,
        compiler_params=pltpu.CompilerParams(vmem_limit_bytes=60 * MIB),
        cost_estimate=pl.CostEstimate(flops=10 * tokens * columns, bytes_accessed=9 * tokens * columns, transcendentals=0),
        name="turn",
    )(where, proj, gain, cosine, sine)


def rope_tables(cell_ids):
    half_head = HEAD // 2
    sixth_head = HEAD // 6
    frame_pairs = half_head - 2 * sixth_head
    lane = jnp.arange(HEAD, dtype=jnp.int32)
    pair_index = lane // 2
    in_frame = pair_index < frame_pairs
    in_height = jnp.logical_and(pair_index >= frame_pairs, pair_index < frame_pairs + sixth_head)
    local_index = jnp.where(
        in_frame,
        pair_index,
        jnp.where(in_height, pair_index - frame_pairs, pair_index - frame_pairs - sixth_head),
    )
    section = jnp.where(in_frame, frame_pairs, sixth_head)
    frequency = jnp.power(10000.0, -local_index.astype(F32) / section.astype(F32))
    frame_ids = cell_ids // (TILE_H * TILE_W)
    row_ids = cell_ids // TILE_W % TILE_H
    col_ids = cell_ids % TILE_W
    position = jnp.where(
        in_frame[None, :],
        frame_ids[:, None],
        jnp.where(in_height[None, :], row_ids[:, None], col_ids[:, None]),
    )
    angles = position.astype(F32) * frequency[None, :]
    sign = jnp.where(lane % 2 == 0, -1.0, 1.0)
    return jnp.cos(angles), jnp.sin(angles) * sign[None, :]


def on_device(
    context,
    main_stream,
    cell_order,
    modulation,
    hint_weight,
    hint_bias,
    weights,
    biases,
    norm_gains,
):
    branch = lax.axis_index("branch")
    seq = lax.axis_index("seq")
    dp = lax.axis_index("dp")
    y, x = seq // NX, seq % NX
    hh = dp // NZ
    where = jnp.stack(
        [((y + dy) % NY) * NX + (x + dx) % NX for dy, dx in REL] + [branch, seq, hh]
    ).astype(jnp.int32)

    tokens, features = main_stream.shape[1:]
    width = features // NS
    part = tokens // 2
    rows = NS * part
    lines = rows // 128

    def along_z(x):
        return lax.all_gather(x, "dp", axis=0, axis_index_groups=Z_GROUPS)

    hint_weights = along_z(cat(hint_weight, dp_send(hint_weight, 1, 0)))
    slot = weights[0]

    def join_slot(other):
        return jnp.where(hh == 0, cat(slot, other), cat(other, slot))

    blocks, slot_both, main_half, where = relay_context(
        context[0], dp_send(slot, 1, 0), join_slot, split_columns(where, main_stream[0]), where
    )
    weight = along_z(slot_both)
    main_cols = lax.all_to_all(main_half, "seq", split_axis=0, concat_axis=0, tiled=True).reshape(rows, width)

    sent, kept = hint_matmul(where, blocks, hint_weights)
    sent, main_cols = lax.optimization_barrier((sent, main_cols))
    got = core_swap(sent)
    mixed, small = mix(kept, got, main_cols, hint_bias[None, :], cell_order)

    cut_a, cut_b = thirds(rows)
    back, ahead, beside, small = lax.optimization_barrier(
        (
            seq_send(mixed, 1, 0),
            seq_send(mixed, -1, 0),
            seq_send(mixed, 0, 1),
            lax.all_to_all(small, "seq", split_axis=0, concat_axis=0, tiled=True),
        )
    )
    far, ahead_beside, back_beside = seq_send(back, 1, 0), seq_send(beside, -1, 0), seq_send(back, 0, 1)
    means = small[:, 0:lines].reshape(NS, rows)
    spreads = small[:, lines : 2 * lines].reshape(NS, rows)
    average = jnp.mean(means, axis=0)
    apart = means - average[None, :]
    variance = (jnp.sum(spreads, axis=0) + width * jnp.sum(apart * apart, axis=0)) / features
    norm_rows = cat(average[None], lax.rsqrt(variance + norm_eps)[None], jnp.zeros((6, rows), F32))
    cells = small[:, 2 * lines].reshape(NS * tokens).astype(jnp.int32)
    mod = jnp.transpose(modulation[0].reshape(2, NS, width), (1, 0, 2))
    first, first_next = norm(
        where, norm_rows, mod, [mixed, back, ahead, beside], [(i, i, 0, 0, rows) for i in range(4)]
    )
    tables = rope_tables(cells)
    far, ahead_beside, back_beside, tables = lax.optimization_barrier((far, ahead_beside, back_beside, tables))
    first_got = core_swap(first)
    last = [
        seq_send(far[:cut_a], 0, 1),
        seq_send(back_beside[cut_a:cut_b], 1, 0),
        seq_send(ahead_beside[cut_b:], -1, 0),
    ]
    second, second_next = norm(
        where, norm_rows, mod, [far, ahead_beside, back_beside], [(4 + i, i, 0, 0, rows) for i in range(3)]
    )
    norm_other = core_swap(after(norm_rows, far))
    last, second, norm_other = lax.optimization_barrier((last, second, norm_other))
    second_got = core_swap(second)
    last_got = [core_swap(piece) for piece in last]
    next_half = next_rows(where, first_next, second_next, last)

    weight = after(weight, last, next_half)
    proj, squares = project(
        where, [first, second, *last], [first_got, second_got, *last_got], weight, biases, norm_rows, norm_other, mod
    )
    squares = lax.all_to_all(squares, "seq", split_axis=0, concat_axis=0, tiled=True)
    turned = turn(where, proj, norm_gains, *tables)

    next_mine = lax.dynamic_index_in_dim(next_half, branch, 0, keepdims=False)
    next_sent = lax.dynamic_index_in_dim(next_half, 1 - branch, 0, keepdims=False)
    next_got = core_swap(next_sent)
    main_next = jnp.where(branch == 0, cat(next_mine, next_got), cat(next_got, next_mine))

    squares, main_next, turned = lax.optimization_barrier((squares, main_next, turned))
    inv_rms = lax.rsqrt(jnp.sum(squares, axis=0) / features + norm_eps).reshape(2, NS, part)
    inv_rms = jnp.where(branch == 0, inv_rms, inv_rms[::-1])
    inv_rms = jnp.transpose(inv_rms, (1, 0, 2)).reshape(NS * tokens)
    rotated = (turned * inv_rms[:, None]).astype(BF16)
    return (rotated[None, None], main_next[None])


def solution(mesh):
    placed = (
        P("dp", "seq", "branch"),
        P("dp", "seq", None),
        P("dp", "seq"),
        P("dp", None, None),
        P(("branch", "dp"), "seq"),
        P("seq"),
        P("branch", "dp", "seq"),
        P("branch", "seq"),
        P("branch", "seq"),
    )
    return jax.shard_map(
        on_device,
        mesh=mesh,
        in_specs=placed,
        out_specs=(P("branch", "dp", None, "seq"), P("dp", "seq", "branch")),
        check_vma=False,
    )
```

```python
import functools

import jax
import jax.numpy as jnp
from jax import lax
from jax.experimental import pallas as pl
from jax.experimental.pallas import tpu as pltpu
from jax.sharding import PartitionSpec as P

HEAD = 128
TILE_H = 8
TILE_W = 16
norm_eps = 1e-06

F32 = jnp.float32
BF16 = jnp.bfloat16

NY, NX, NH, NZ = 4, 2, 2, 8
NS = NY * NX
SWAP = [(0, 1), (1, 0)]
REL = [(0, 0), (-1, 0), (1, 0), (0, 1), (2, 0), (1, 1), (-1, 1), (2, 1)]
Z_GROUPS = [[hh * NZ + z for z in range(NZ)] for hh in range(NH)]
MIB = 1024 * 1024

HBM = pl.BlockSpec(memory_space=pltpu.HBM)
WHOLE = pl.BlockSpec(memory_space=pltpu.VMEM)
SMALL = pl.CostEstimate(flops=1, bytes_accessed=1, transcendentals=0)
SCALARS = pl.BlockSpec(memory_space=pltpu.SMEM)


def seq_pairs(dy, dx):
    return [(s, ((s // NX + dy) % NY) * NX + (s % NX ^ dx)) for s in range(NS)]


def dp_pairs(dh, dz):
    return [(d, (d // NZ ^ dh) * NZ + (d % NZ + dz) % NZ) for d in range(NH * NZ)]


def seq_send(x, dy, dx):
    return lax.ppermute(x, "seq", seq_pairs(dy, dx))


def dp_send(x, dh, dz):
    return lax.ppermute(x, "dp", dp_pairs(dh, dz))


def core_swap(x):
    return lax.ppermute(x, "branch", SWAP)


def thirds(rows):
    unit = rows // NS
    return 3 * unit, 5 * unit


def after(value, *earlier):
    return lax.optimization_barrier((value, earlier))[0]


def cat(*parts):
    return jnp.concatenate(parts, 0)


def split_kernel(where_ref, main_ref, out_ref):
    tokens, width = out_ref.shape[1:]
    at = pl.ds(pl.multiple_of(where_ref[8] * tokens, 16), tokens)
    for s in range(NS):
        out_ref[s] = main_ref[at, s * width : (s + 1) * width]


def split_columns(where, main):
    tokens, features = main.shape
    return pl.pallas_call(
        split_kernel,
        out_shape=jax.ShapeDtypeStruct((NS, tokens // 2, features // NS), main.dtype),
        in_specs=[SCALARS, WHOLE],
        out_specs=WHOLE,
        compiler_params=pltpu.CompilerParams(vmem_limit_bytes=16 * MIB),
        cost_estimate=SMALL,
        name="split_columns",
    )(where, main)


def relay_context(own, slot_other, join_slot, main_half, where):
    back, ahead, slot_other = lax.optimization_barrier((seq_send(own, 1, 0), seq_send(own, -1, 0), slot_other))
    far, beside, slot_both = lax.optimization_barrier(
        (seq_send(back, 1, 0), seq_send(after(own, back), 0, 1), join_slot(slot_other))
    )
    ahead_beside, back_beside, far_beside, main_half, where = lax.optimization_barrier(
        (seq_send(beside, -1, 0), seq_send(beside, 1, 0), seq_send(far, 0, 1), main_half, where)
    )
    return [own, back, ahead, beside, far, ahead_beside, back_beside, far_beside], slot_both, main_half, where


def hint_kernel(rows, where_ref, weight_ref, *refs):
    blocks = refs[:NS]
    other_ref, mine_ref, ctx, wgt, sem = refs[NS:]
    half_rows = rows // 2
    depth = weight_ref.shape[1] // NH
    mine, column = where_ref[8], where_ref[10]
    copies = []

    def copy(src, dst):
        c = pltpu.make_async_copy(src, dst, sem.at[len(copies)])
        c.start()
        copies.append(c)

    def tokens(half, slot):
        for i, block in enumerate(blocks):
            src = pl.ds(pl.multiple_of(half * half_rows, 16), half_rows)
            copy(block.at[src], ctx.at[slot, pl.ds(pl.multiple_of(where_ref[i] * half_rows, 16), half_rows)])

    def column_rows(col):
        first = jnp.where(col == column, 0, depth)
        for z in range(NZ):
            src = pl.ds(pl.multiple_of(first, 16), depth)
            copy(weight_ref.at[z, src], wgt.at[pl.ds((col * NZ + z) * depth, depth)])

    tokens(1 - mine, 0)
    column_rows(0)
    column_rows(1)
    tokens(mine, 1)
    deep = NZ * depth
    done = 0
    for count, out_ref, slot, k in ((NS + NZ, other_ref, 0, 0), (NZ, other_ref, 0, 1), (NS, mine_ref, 1, None)):
        for c in copies[done : done + count]:
            c.wait()
        done += count
        if k is None:
            out_ref[...] = jnp.dot(ctx[slot], wgt[...], preferred_element_type=F32)
        else:
            lanes = slice(k * deep, (k + 1) * deep)
            product = jnp.dot(ctx[slot, :, lanes], wgt[lanes, :], preferred_element_type=F32)
            out_ref[...] = out_ref[...] + product if k else product


def hint_matmul(where, blocks, weight):
    rows, features = blocks[0].shape
    columns = weight.shape[2]
    half = NS * rows // 2
    return pl.pallas_call(
        functools.partial(hint_kernel, rows),
        out_shape=[jax.ShapeDtypeStruct((half, columns), F32)] * 2,
        in_specs=[SCALARS] + [HBM] * (1 + NS),
        out_specs=[WHOLE] * 2,
        scratch_shapes=[
            pltpu.VMEM((2, half, features), BF16),
            pltpu.VMEM((features, columns), BF16),
            pltpu.SemaphoreType.DMA((2 * NS + NH * NZ,)),
        ],
        compiler_params=pltpu.CompilerParams(vmem_limit_bytes=60 * MIB),
        cost_estimate=SMALL,
        name="hint",
    )(where, weight, *blocks)


def mix_kernel(keep_ref, got_ref, main_ref, bias_ref, cell_ref, mixed_ref, small_ref):
    rows = keep_ref.shape[0]
    lines = rows // 128
    hint = (keep_ref[...] + got_ref[...] + bias_ref[...]).astype(BF16)
    mixed = (main_ref[...].astype(F32) + hint.astype(F32)).astype(BF16)
    mixed_ref[...] = mixed
    values = mixed.astype(F32)
    average = jnp.mean(values, axis=-1, keepdims=True)
    centered = values - average
    spread = jnp.sum(centered * centered, axis=-1, keepdims=True)
    lane = lax.broadcasted_iota(jnp.int32, (rows, 128), 1)
    both = jnp.where(lane == 0, average, spread).T
    cells = jnp.broadcast_to(cell_ref[...].astype(F32), (8, 128))
    for d in range(NS):
        for r in range(2):
            for k in range(lines):
                small_ref[d, r * lines + k : r * lines + k + 1, :] = both[r : r + 1, k * 128 : (k + 1) * 128]
        small_ref[d, 2 * lines :, :] = cells


def mix(keep, got, main_cols, bias, cells):
    rows, columns = keep.shape
    return pl.pallas_call(
        mix_kernel,
        out_shape=[
            jax.ShapeDtypeStruct((rows, columns), BF16),
            jax.ShapeDtypeStruct((NS, 2 * rows // 128 + 8, 128), F32),
        ],
        compiler_params=pltpu.CompilerParams(vmem_limit_bytes=16 * MIB),
        cost_estimate=SMALL,
        name="mix",
    )(keep, got, main_cols, bias, cells)


def norm_kernel(rows, width, order, pieces, where_ref, norm_ref, mod_ref, *refs):
    mean, rstd, xs, sem = refs[-4:]
    normed_ref, next_ref = refs[-6:-4]
    arrays = refs[:-6]
    copies = []
    for k, (block, array, first, lo, hi) in enumerate(pieces):
        src, dst = arrays[array].at[pl.ds(first, hi - lo)], xs.at[order.index(block), pl.ds(lo, hi - lo)]
        c = pltpu.make_async_copy(src, dst, sem.at[k])
        c.start()
        copies.append(c)
    mean[...] = jnp.broadcast_to(norm_ref[0:1, :], (128, rows)).T
    rstd[...] = jnp.broadcast_to(norm_ref[1:2, :], (128, rows)).T
    for c in copies:
        c.wait()
    step = 128
    tokens = rows // NS
    me = pl.ds(pl.multiple_of(where_ref[9] * tokens, 16), tokens)
    for j, block in enumerate(order):
        s = where_ref[block]
        shift, scale = mod_ref[s, 0:1, :], 1.0 + mod_ref[s, 1:2, :]

        def body(i, _, j=j, shift=shift, scale=scale):
            at = pl.ds(pl.multiple_of(i * step, 16), step)
            into = pl.ds(pl.multiple_of(j * rows + i * step, 16), step)
            average, root = mean[at, :], rstd[at, :]
            for a in range(width // 128):
                lanes = slice(a * 128, (a + 1) * 128)
                values = (xs[j, at, lanes].astype(F32) - average) * root
                normed_ref[into, lanes] = (values * scale[:, lanes] + shift[:, lanes]).astype(BF16)
            return 0

        lax.fori_loop(0, rows // step, body, 0)
        next_ref[j] = xs[j, me, :]


def norm(where, norm_rows, mod, arrays, pieces):
    order = sorted({piece[0] for piece in pieces})
    rows, width = norm_rows.shape[1], mod.shape[2]
    tokens = rows // NS
    return pl.pallas_call(
        functools.partial(norm_kernel, rows, width, order, pieces),
        out_shape=[
            jax.ShapeDtypeStruct((len(order) * rows, width), BF16),
            jax.ShapeDtypeStruct((len(order), tokens, width), BF16),
        ],
        in_specs=[SCALARS, WHOLE, WHOLE] + [HBM] * len(arrays),
        out_specs=[WHOLE] * 2,
        scratch_shapes=[
            pltpu.VMEM((rows, 128), F32),
            pltpu.VMEM((rows, 128), F32),
            pltpu.VMEM((len(order), rows, width), BF16),
            pltpu.SemaphoreType.DMA((len(pieces),)),
        ],
        compiler_params=pltpu.CompilerParams(vmem_limit_bytes=60 * MIB),
        cost_estimate=SMALL,
        name="norm",
    )(where, norm_rows, mod, *arrays)


def next_kernel(where_ref, first_ref, second_ref, *refs):
    pieces, out_ref, whole = refs[:-2], refs[-2], refs[-1]
    tokens, width = first_ref.shape[1:]

    def put(block, part):
        s = where_ref[block]
        out_ref[s // NY, :, pl.ds(pl.multiple_of((s % NY) * width, 128), width)] = part

    count = first_ref.shape[0]
    for j in range(count):
        put(j, first_ref[j])
    for j in range(second_ref.shape[0]):
        put(count + j, second_ref[j])
    at = 0
    for ref in pieces:
        whole[at : at + ref.shape[0], :] = ref[...]
        at += ref.shape[0]
    put(NS - 1, whole[pl.ds(pl.multiple_of(where_ref[9] * tokens, 16), tokens), :])


def next_rows(where, first, second, last):
    tokens, width = first.shape[1:]
    return pl.pallas_call(
        next_kernel,
        out_shape=jax.ShapeDtypeStruct((2, tokens, NY * width), BF16),
        in_specs=[SCALARS] + [WHOLE] * (2 + len(last)),
        out_specs=WHOLE,
        scratch_shapes=[pltpu.VMEM((sum(piece.shape[0] for piece in last), width), BF16)],
        compiler_params=pltpu.CompilerParams(vmem_limit_bytes=16 * MIB),
        cost_estimate=SMALL,
        name="next_rows",
    )(where, first, second, *last)


def project_kernel(counts, cuts, where_ref, *refs):
    sets = len(counts) + len(cuts) - 2
    mine, other = refs[:sets], refs[sets : 2 * sets]
    w_ref, bias_ref, norm_ref, norm_other_ref, mod_ref, out_ref, squares_ref = refs[2 * sets : 2 * sets + 7]
    xs, wgt, raw, mean, rstd, sem_x, sem_w = refs[2 * sets + 7 :]
    rows = out_ref.shape[0] // 2
    width = wgt.shape[0] // NS
    deep = width // 2
    copies = []
    i = 0
    for count, a, b in zip(counts, mine, other):
        for j in range(count):
            src, lanes = pl.ds(j * rows, rows), pl.ds(i * width, width)
            s = where_ref[i]
            z, h = lax.rem(2 * s, NZ), lax.div(2 * s, NZ)
            from_w = pl.ds(pl.multiple_of(h * deep, 16), deep)
            copies.append(
                [
                    pltpu.make_async_copy(w_ref.at[z, from_w], wgt.at[pl.ds(i * width, deep)], sem_w.at[i, 0]),
                    pltpu.make_async_copy(
                        w_ref.at[z + 1, from_w], wgt.at[pl.ds(i * width + deep, deep)], sem_w.at[i, 1]
                    ),
                ]
            )
            if i < NS - 1:
                copies[i] += [
                    pltpu.make_async_copy(a.at[src], xs.at[pl.ds(0, rows), lanes], sem_x.at[2 * i]),
                    pltpu.make_async_copy(b.at[src], xs.at[pl.ds(rows, rows), lanes], sem_x.at[2 * i + 1]),
                ]
            i += 1
    raw_copies = [
        pltpu.make_async_copy(
            refs[side * sets + len(counts) - 1 + k],
            raw.at[pl.ds(side * rows + cuts[k], cuts[k + 1] - cuts[k])],
            sem_x.at[2 * NS + side * (len(cuts) - 1) + k],
        )
        for side in range(2)
        for k in range(len(cuts) - 1)
    ]

    def start(i):
        for c in copies[i] + copies[i + 1]:
            c.start()

    start(0)
    for c in raw_copies:
        c.start()
    start(2)
    for part, ref in enumerate((norm_ref, norm_other_ref)):
        at = pl.ds(part * rows, rows)
        mean[at, :] = jnp.broadcast_to(ref[0:1, :], (128, rows)).T
        rstd[at, :] = jnp.broadcast_to(ref[1:2, :], (128, rows)).T
    s = where_ref[NS - 1]
    shift, scale = mod_ref[s, 0:1, :], 1.0 + mod_ref[s, 1:2, :]
    sums = []
    for i in range(0, NS, 2):
        for c in copies[i] + copies[i + 1]:
            c.wait()
        if i + 4 < NS:
            start(i + 4)
        if i == NS - 2:
            for c in raw_copies:
                c.wait()
            for a in range(width // 128):
                lanes = slice(a * 128, (a + 1) * 128)
                values = (raw[:, lanes].astype(F32) - mean[...]) * rstd[...]
                xs[:, (NS - 1) * width + a * 128 : (NS - 1) * width + (a + 1) * 128] = (
                    values * scale[:, lanes] + shift[:, lanes]
                ).astype(BF16)
        deep_lanes = pl.ds(i * width, 2 * width)
        for part in range(2):
            at = pl.ds(part * rows, rows)
            product = jnp.dot(xs[at, deep_lanes], wgt[deep_lanes, :], preferred_element_type=F32)
            if i == 0:
                out_ref[at, :] = product + bias_ref[...]
            elif i < NS - 2:
                out_ref[at, :] += product
            else:
                values = out_ref[at, :] + product
                out_ref[at, :] = values
                sums.append(jnp.sum(values * values, axis=-1, keepdims=True))
    lane = lax.broadcasted_iota(jnp.int32, (rows, 128), 1)
    both = jnp.where(lane == 0, sums[0], sums[1]).T
    lines = rows // 128
    for d in range(NS):
        for r in range(2):
            for k in range(lines):
                squares_ref[d, r * lines + k : r * lines + k + 1, :] = both[r : r + 1, k * 128 : (k + 1) * 128]


def project(where, mine, other, weight, bias, norm_rows, norm_other, mod):
    width, columns = mine[0].shape[1], weight.shape[2]
    counts = [4, 3, 1]
    rows = mine[0].shape[0] // counts[0]
    cuts = [0, *thirds(rows), rows]
    operands = [*mine, *other, weight]
    return pl.pallas_call(
        functools.partial(project_kernel, counts, cuts),
        out_shape=[
            jax.ShapeDtypeStruct((2 * rows, columns), F32),
            jax.ShapeDtypeStruct((NS, 2 * rows // 128, 128), F32),
        ],
        in_specs=[SCALARS] + [HBM] * len(operands) + [WHOLE] * 4,
        out_specs=[WHOLE] * 2,
        scratch_shapes=[
            pltpu.VMEM((2 * rows, NS * width), BF16),
            pltpu.VMEM((NS * width, columns), BF16),
            pltpu.VMEM((2 * rows, width), BF16),
            pltpu.VMEM((2 * rows, 128), F32),
            pltpu.VMEM((2 * rows, 128), F32),
            pltpu.SemaphoreType.DMA((2 * NS + 2 * len(cuts),)),
            pltpu.SemaphoreType.DMA((NS, 2)),
        ],
        compiler_params=pltpu.CompilerParams(vmem_limit_bytes=60 * MIB),
        cost_estimate=pl.CostEstimate(
            flops=4 * rows * NS * width * columns,
            bytes_accessed=2 * NS * width * (2 * rows + columns) + 8 * rows * columns,
            transcendentals=0,
        ),
        name="project",
    )(where, *operands, bias, norm_rows, norm_other, mod)


def turn_kernel(
    where_ref, proj_ref, next_ref, got_ref, gain_ref, cos_ref, sin_ref, out_ref, placed_ref,
    held, done, near, load_sem, store_sem, near_sem,
):
    chunks, step, columns = held.shape
    part = proj_ref.shape[0] // 2 // NS
    loads = [pltpu.make_async_copy(proj_ref.at[pl.ds(k * step, step)], held.at[k], load_sem.at[k]) for k in range(chunks)]
    for c in loads:
        c.start()
    mine = where_ref[8]
    tokens = near.shape[1]
    fetches, places = [], []
    for h, (src, half) in enumerate(((next_ref.at[mine], mine), (got_ref, 1 - mine))):
        at = pl.ds(pl.multiple_of(half * tokens, 16), tokens)
        fetches.append(pltpu.make_async_copy(src, near.at[h], near_sem.at[h]))
        places.append(pltpu.make_async_copy(near.at[h], placed_ref.at[at], near_sem.at[2 + h]))
    for c in fetches:
        c.start()
    even = lax.broadcasted_iota(jnp.int32, (part, HEAD), 1) % 2 == 0
    stores = []
    for k in range(chunks):
        half = mine if k < chunks // 2 else 1 - mine
        if k == chunks // 2:
            for fetch, place in zip(fetches, places):
                fetch.wait()
                place.start()
        loads[k].wait()
        for j in range(step // part):
            s = k % (chunks // 2) * (step // part) + j
            src = slice(j * part, (j + 1) * part)
            dst = pl.ds(pl.multiple_of((2 * s + half) * part, 16), part)
            cosine, sine = cos_ref[dst, :], sin_ref[dst, :]
            for a in range(columns // HEAD):
                lanes = slice(a * HEAD, (a + 1) * HEAD)
                value = held[k, src, lanes] * gain_ref[:, lanes]
                partner = jnp.where(even, pltpu.roll(value, HEAD - 1, 1), pltpu.roll(value, 1, 1))
                done[k, src, lanes] = value * cosine + partner * sine
            c = pltpu.make_async_copy(done.at[k, pl.ds(j * part, part)], out_ref.at[dst], store_sem.at[len(stores)])
            c.start()
            stores.append(c)
    for c in stores + places:
        c.wait()


def turn(where, proj, next_half, next_got, gain, cosine, sine):
    tokens, columns = proj.shape
    chunks = 8
    return pl.pallas_call(
        turn_kernel,
        out_shape=[
            jax.ShapeDtypeStruct((tokens, columns), F32),
            jax.ShapeDtypeStruct((2 * next_got.shape[0], next_got.shape[1]), BF16),
        ],
        in_specs=[SCALARS] + [HBM] * 3 + [WHOLE] * 3,
        out_specs=[HBM] * 2,
        scratch_shapes=[
            pltpu.VMEM((chunks, tokens // chunks, columns), F32),
            pltpu.VMEM((chunks, tokens // chunks, columns), F32),
            pltpu.VMEM((2, *next_got.shape), BF16),
            pltpu.SemaphoreType.DMA((chunks,)),
            pltpu.SemaphoreType.DMA((2 * NS,)),
            pltpu.SemaphoreType.DMA((4,)),
        ],
        compiler_params=pltpu.CompilerParams(vmem_limit_bytes=60 * MIB),
        cost_estimate=pl.CostEstimate(flops=10 * tokens * columns, bytes_accessed=9 * tokens * columns, transcendentals=0),
        name="turn",
    )(where, proj, next_half, next_got, gain, cosine, sine)


def rope_tables(cell_ids):
    half_head = HEAD // 2
    sixth_head = HEAD // 6
    frame_pairs = half_head - 2 * sixth_head
    lane = jnp.arange(HEAD, dtype=jnp.int32)
    pair_index = lane // 2
    in_frame = pair_index < frame_pairs
    in_height = jnp.logical_and(pair_index >= frame_pairs, pair_index < frame_pairs + sixth_head)
    local_index = jnp.where(
        in_frame,
        pair_index,
        jnp.where(in_height, pair_index - frame_pairs, pair_index - frame_pairs - sixth_head),
    )
    section = jnp.where(in_frame, frame_pairs, sixth_head)
    frequency = jnp.power(10000.0, -local_index.astype(F32) / section.astype(F32))
    frame_ids = cell_ids // (TILE_H * TILE_W)
    row_ids = cell_ids // TILE_W % TILE_H
    col_ids = cell_ids % TILE_W
    position = jnp.where(
        in_frame[None, :],
        frame_ids[:, None],
        jnp.where(in_height[None, :], row_ids[:, None], col_ids[:, None]),
    )
    angles = position.astype(F32) * frequency[None, :]
    sign = jnp.where(lane % 2 == 0, -1.0, 1.0)
    return jnp.cos(angles), jnp.sin(angles) * sign[None, :]


def on_device(
    context,
    main_stream,
    cell_order,
    modulation,
    hint_weight,
    hint_bias,
    weights,
    biases,
    norm_gains,
):
    branch = lax.axis_index("branch")
    seq = lax.axis_index("seq")
    dp = lax.axis_index("dp")
    y, x = seq // NX, seq % NX
    hh = dp // NZ
    where = jnp.stack(
        [((y + dy) % NY) * NX + (x + dx) % NX for dy, dx in REL] + [branch, seq, hh]
    ).astype(jnp.int32)

    tokens, features = main_stream.shape[1:]
    width = features // NS
    part = tokens // 2
    rows = NS * part
    lines = rows // 128

    def along_z(x):
        return lax.all_gather(x, "dp", axis=0, axis_index_groups=Z_GROUPS)

    hint_weights = along_z(cat(hint_weight, dp_send(hint_weight, 1, 0)))
    slot = weights[0]

    def join_slot(other):
        return jnp.where(hh == 0, cat(slot, other), cat(other, slot))

    blocks, slot_both, main_half, where = relay_context(
        context[0], dp_send(slot, 1, 0), join_slot, split_columns(where, main_stream[0]), where
    )
    weight = along_z(slot_both)
    main_cols = lax.all_to_all(main_half, "seq", split_axis=0, concat_axis=0, tiled=True).reshape(rows, width)

    sent, kept = hint_matmul(where, blocks, hint_weights)
    sent, main_cols = lax.optimization_barrier((sent, main_cols))
    got = core_swap(sent)
    mixed, small = mix(kept, got, main_cols, hint_bias[None, :], cell_order)

    cut_a, cut_b = thirds(rows)
    back, ahead, beside, small = lax.optimization_barrier(
        (
            seq_send(mixed, 1, 0),
            seq_send(mixed, -1, 0),
            seq_send(mixed, 0, 1),
            lax.all_to_all(small, "seq", split_axis=0, concat_axis=0, tiled=True),
        )
    )
    far, ahead_beside, back_beside = seq_send(back, 1, 0), seq_send(beside, -1, 0), seq_send(back, 0, 1)
    means = small[:, 0:lines].reshape(NS, rows)
    spreads = small[:, lines : 2 * lines].reshape(NS, rows)
    average = jnp.mean(means, axis=0)
    apart = means - average[None, :]
    variance = (jnp.sum(spreads, axis=0) + width * jnp.sum(apart * apart, axis=0)) / features
    norm_rows = cat(average[None], lax.rsqrt(variance + norm_eps)[None], jnp.zeros((6, rows), F32))
    cells = small[:, 2 * lines].reshape(NS * tokens).astype(jnp.int32)
    mod = jnp.transpose(modulation[0].reshape(2, NS, width), (1, 0, 2))
    first, first_next = norm(
        where, norm_rows, mod, [mixed, back, ahead, beside], [(i, i, 0, 0, rows) for i in range(4)]
    )
    tables = rope_tables(cells)
    far, ahead_beside, back_beside, tables = lax.optimization_barrier((far, ahead_beside, back_beside, tables))
    first_got = core_swap(first)
    last = [
        seq_send(far[:cut_a], 0, 1),
        seq_send(back_beside[cut_a:cut_b], 1, 0),
        seq_send(ahead_beside[cut_b:], -1, 0),
    ]
    second, second_next = norm(
        where, norm_rows, mod, [far, ahead_beside, back_beside], [(4 + i, i, 0, 0, rows) for i in range(3)]
    )
    norm_other = core_swap(after(norm_rows, far))
    last, second, norm_other = lax.optimization_barrier((last, second, norm_other))
    second_got = core_swap(second)
    last_got = [core_swap(piece) for piece in last]
    next_half = next_rows(where, first_next, second_next, last)

    weight = after(weight, last, next_half)
    proj, squares = project(
        where, [first, second, *last], [first_got, second_got, *last_got], weight, biases, norm_rows, norm_other, mod
    )
    squares = lax.all_to_all(squares, "seq", split_axis=0, concat_axis=0, tiled=True)

    next_sent = lax.dynamic_index_in_dim(next_half, 1 - branch, 0, keepdims=False)
    turned, main_next = turn(where, proj, next_half, core_swap(next_sent), norm_gains, *tables)

    squares, turned = lax.optimization_barrier((squares, turned))
    inv_rms = lax.rsqrt(jnp.sum(squares, axis=0) / features + norm_eps).reshape(2, NS, part)
    inv_rms = jnp.where(branch == 0, inv_rms, inv_rms[::-1])
    inv_rms = jnp.transpose(inv_rms, (1, 0, 2)).reshape(NS * tokens)
    rotated = (turned * inv_rms[:, None]).astype(BF16)
    return (rotated[None, None], main_next[None])


def solution(mesh):
    placed = (
        P("dp", "seq", "branch"),
        P("dp", "seq", None),
        P("dp", "seq"),
        P("dp", None, None),
        P(("branch", "dp"), "seq"),
        P("seq"),
        P("branch", "dp", "seq"),
        P("branch", "seq"),
        P("branch", "seq"),
    )
    return jax.shard_map(
        on_device,
        mesh=mesh,
        in_specs=placed,
        out_specs=(P("branch", "dp", None, "seq"), P("dp", "seq", "branch")),
        check_vma=False,
    )
```
